256 devices in a mesh: grp: 4 (over z_lo), tile: 32 (over x, y, z_hi), cores: 2 (over core).
Axes of the slice: x: 4, y: 4, z: 8 (z_hi: 2, z_lo: 4; z = z_hi * 4 + z_lo), core: 2. Of those that a mesh axis runs over, the one named last changes fastest.
Arguments:
- trial_collection: float32 [32, 3, 1024, 1024], P('grp', None, 'tile', 'cores'), may hold values from -6 to 6
- seabed_profile: float32 [1024, 1024], P('tile', 'cores'), may hold values from 0.4 to 1.8
- observed: float32 [4096], P(('grp', 'tile', 'cores')), may hold values from -6 to 6
- variances: float32 [4096], P(('grp', 'tile', 'cores')), may hold values from 4 to 40
- perturbations: float32 [4096, 32], P(('grp', 'tile', 'cores')), may hold values from -6 to 6
- stencil_cells: int32 [4096, 4], P(('grp', 'tile', 'cores')), may hold values from 0 to 4095, as said below
- stencil_weights: float32 [4096, 4], P(('grp', 'tile', 'cores')), may hold values from 0.1 to 0.5
- region_mask: int32 [4096, 8], P(('grp', 'tile', 'cores')), may hold values from 0 to 1, as said below
Outputs:
- propagated_trials: float32 [32, 3, 1024, 1024], P('grp', None, 'tile', 'cores')
- analysis_updates: float32 [32, 3, 1024, 1024], P('grp', None, 'tile', 'cores')
The draws below stay inside these ranges and needn't reach their ends.
Inputs may be any that keep to these rules, and one draw needn't show every extreme that they name: `stencil_cells`: each observation's four entries are s, s + 1, s + 512, s + 513 for a cell s of its block in a row below 7 and a column below 511; in every block the first observation has s = 3582 and the second s = 0. `region_mask`: an observation counts in the region that holds its block's rows, in each region next to that one or not, and in no other.
All inputs are finite; a program needn't handle non-finite values.
Results may differ from the reference program's by a relative error of at most 0.00018.
Values sent between devices are 32-bit elements; how exact they have to be, the bound alone decides.
No kernel may reach another device: no remote copies, remote signals or barrier semaphores. Data moves between devices by JAX's collectives and lax.ppermute only.
A program may use at most 64 MiB of HBM per device.

```python
import math
import jax
import jax.numpy as jnp
from jax import lax

E = 32
CX = 32
NY = 1024
STEPS = 3
REG = 8
OBS_DEV = 16
CY = 512
XA = 8
NX = 1024
ROWS_REGION = 128
NOBS = 4096
N_TILE = 32
N_CORES = 2


def draw_stencil_cells(key, part):
    key = jax.random.fold_in(key, 11)
    first_key, second_key = jax.random.split(key)
    base_row = jax.random.randint(first_key, (NOBS,), 0, XA - 1)
    base_col = jax.random.randint(second_key, (NOBS,), 0, CY - 1)
    rank_in_block = jnp.arange(NOBS, dtype=jnp.int32) % OBS_DEV
    base_row = jnp.where(rank_in_block == 0, XA - 2, jnp.where(rank_in_block == 1, 0, base_row))
    base_col = jnp.where(rank_in_block == 0, CY - 2, jnp.where(rank_in_block == 1, 0, base_col))
    anchor = base_row * CY + base_col
    return jnp.stack([anchor, anchor + 1, anchor + CY, anchor + CY + 1], axis=1).astype(jnp.int32)


def draw_region_mask(key, part):
    key = jax.random.fold_in(key, 12)
    device = jnp.arange(NOBS, dtype=jnp.int32) // OBS_DEV
    group_id = device // (N_TILE * N_CORES)
    tile_id = device // N_CORES % N_TILE
    own_region = (tile_id * CX + group_id * XA) // ROWS_REGION
    coins = jax.random.randint(key, (NOBS, REG), 0, 2)
    distance = jnp.abs(jnp.arange(REG, dtype=jnp.int32)[None, :] - own_region[:, None])
    return jnp.where(distance == 0, 1, jnp.where(distance == 1, coins, 0)).astype(jnp.int32)


def steps_of(key, extent, cuts, least, top_value):
    loudness, own = 1.0, jax.random.fold_in(key, 6)
    for position, shards_of in cuts:
        steps = jnp.exp(jax.random.uniform(jax.random.fold_in(own, position), (shards_of,), jnp.float32, least / len(cuts), top_value / len(cuts)))
        loudness = loudness * jnp.repeat(steps, extent[position] // shards_of).reshape([-1 if axis == position else 1 for axis in range(len(extent))])
    return loudness


def normal_values(stream_key, extent, width, bound, cuts=(), held_as=jnp.bfloat16):
    loudness = steps_of(stream_key, extent, cuts, -0.22, 0.18) if cuts else 1.0
    drawn = jax.random.normal(stream_key, extent, jnp.float32) * width * loudness
    return jnp.minimum(jnp.maximum(drawn, -bound), bound).astype(held_as)


def setup_inputs(seed: int = 0) -> dict:
    keys = jax.random.split(jax.random.key(seed), 9)
    return {
        "trial_collection": normal_values(keys[0], (E, 3, NX, NY), 1.0, 6.0, ((0, 4), (2, 32), (3, 2)), jnp.float32),
        "seabed_profile": jnp.clip(jnp.exp(math.log(1.8) - 1.50407736 * jax.random.uniform(keys[1], (NX, NY), jnp.float32) ** steps_of(keys[1], (NX, NY), ((0, 32), (1, 2)), -0.2, 0.2)), 0.4, 1.8),
        "observed": normal_values(keys[2], (NOBS,), 1.0, 6.0, ((0, 256),), jnp.float32),
        "variances": jnp.clip(jnp.exp(math.log(40.0) - 2.3025851 * jax.random.uniform(keys[3], (NOBS,), jnp.float32) ** steps_of(keys[3], (NOBS,), ((0, 256),), -0.2, 0.2)), 4.0, 40.0),
        "perturbations": normal_values(keys[4], (NOBS, E), 1.0, 6.0, ((0, 256),), jnp.float32),
        "stencil_cells": draw_stencil_cells(jax.random.fold_in(keys[8], 71), 0),
        "stencil_weights": jnp.clip(0.1 + 0.4 * jax.random.uniform(keys[6], (NOBS, 4), jnp.float32) ** steps_of(keys[6], (NOBS, 4), ((0, 256),), -0.2, 0.2), 0.1, 0.5),
        "region_mask": draw_region_mask(jax.random.fold_in(keys[8], 71), 0),
    }


FRICTION = 0.02
HIGHEST = lax.Precision.HIGHEST

def widen(field):
    return jnp.pad(field, ((1, 1), (1, 1)))

def advance(free_elevation, zonal_speed, meridional_speed, seabed_profile):
    flux_east = widen(seabed_profile * zonal_speed)
    flux_north = widen(seabed_profile * meridional_speed)
    spread = 0.5 * (flux_east[2:, 1:-1] - flux_east[:-2, 1:-1]) + 0.5 * (flux_north[1:-1, 2:] - flux_north[1:-1, :-2])
    free_elevation = free_elevation - spread
    padded = widen(free_elevation)
    zonal_speed = (1.0 - FRICTION) * zonal_speed - 0.5 * (padded[2:, 1:-1] - padded[:-2, 1:-1])
    meridional_speed = (1.0 - FRICTION) * meridional_speed - 0.5 * (padded[1:-1, 2:] - padded[1:-1, :-2])
    return (free_elevation, zonal_speed, meridional_speed)

def propagated_trial(model_variables, seabed_profile):
    free_elevation, zonal_speed, meridional_speed = (model_variables[0], model_variables[1], model_variables[2])
    for repeat in range(STEPS):
        free_elevation, zonal_speed, meridional_speed = advance(free_elevation, zonal_speed, meridional_speed, seabed_profile)
    return jnp.stack([free_elevation, zonal_speed, meridional_speed])

def solve_one(triangle, target):
    return jax.scipy.linalg.cho_solve((triangle, True), target)

def transform(products):
    members = products.shape[1]
    system = products[:, :, :members] + (members - 1.0) * jnp.eye(members, dtype=jnp.float32)[None]
    factor = jnp.linalg.cholesky(system)
    return jax.vmap(solve_one)(factor, products[:, :, members:])

def reference(trial_collection, seabed_profile, observed, variances, perturbations, stencil_cells, stencil_weights, region_mask):
    propagated_trials = lax.map(lambda model_variables: propagated_trial(model_variables, seabed_profile), trial_collection)
    ordinal = jnp.arange(NOBS, dtype=jnp.int32)
    device = ordinal // OBS_DEV
    group_id = device // (N_TILE * N_CORES)
    tile_id = device // N_CORES % N_TILE
    core_id = device % N_CORES
    row_start = tile_id * CX + group_id * XA
    mesh_ordinate = (row_start[:, None] + stencil_cells // CY).astype(jnp.int32)
    mesh_abscissa = ((core_id * CY)[:, None] + stencil_cells % CY).astype(jnp.int32)
    picked_components = propagated_trials[:, 0][:, mesh_ordinate, mesh_abscissa]
    observed_state = lax.optimization_barrier(jnp.sum(picked_components * stencil_weights[None], axis=2))
    centre = lax.optimization_barrier(jnp.mean(observed_state, axis=0))
    anomaly_obs = observed_state - centre[None]
    innovation = observed[None] + jnp.sqrt(variances)[None] * perturbations.T - observed_state
    scaled = anomaly_obs / variances[None]
    paired = jnp.concatenate([anomaly_obs, innovation], axis=0)
    products = jnp.einsum('or,eo,go->reg', region_mask.astype(jnp.float32), scaled, paired, precision=HIGHEST)
    weights = transform(products)
    trial_anomalies = propagated_trials - lax.optimization_barrier(jnp.mean(propagated_trials, axis=0, keepdims=True))
    pieces = []
    for region in range(REG):
        block = trial_anomalies[:, :, region * ROWS_REGION:(region + 1) * ROWS_REGION]
        pieces.append(jnp.einsum('fkxy,fe->ekxy', block, weights[region], precision=HIGHEST))
    analysis_updates = jnp.concatenate(pieces, axis=2)
    return (propagated_trials, analysis_updates)
```

```python
import functools

import jax
import jax.numpy as jnp
from jax import lax
from jax.experimental import pallas as pl
from jax.experimental.pallas import tpu as pltpu
from jax.sharding import Mesh, PartitionSpec as P

STEPS = 3
REG = 8
GRP = 4
SUB = 4
MEM = 8
E = 32
CX = 32
CY = 512
LANE = 128
PARTS = CY // LANE
WIDE = CY + LANE
PAD = 8
ROWS = CX + 2 * PAD
OBS = 16
DU, DV, DL = 6, 5, 5
STRIP = DU + DV + DL + 1
FRICTION = 0.02
HIGHEST = lax.Precision.HIGHEST
F32 = jnp.float32
BF16 = jnp.bfloat16
SIDE = ("grp", "sub", "cores")
TILE = ("reg", "sub")


def vmem(n):
    return [pl.BlockSpec(memory_space=pltpu.VMEM)] * n


SMEM = pl.BlockSpec(memory_space=pltpu.SMEM)
PARAMS = pltpu.CompilerParams(vmem_limit_bytes=48 * 1024 * 1024)


def call(body, outs, args, scratch=(), flops=0):
    moved = sum(a.size * 4 for a in args) + sum(4 * o.size for o in outs)
    return pl.pallas_call(
        body,
        out_shape=list(outs),
        in_specs=[SMEM] + vmem(len(args) - 1),
        out_specs=vmem(len(outs)),
        scratch_shapes=list(scratch),
        compiler_params=PARAMS,
        cost_estimate=pl.CostEstimate(flops=flops, bytes_accessed=moved, transcendentals=0),
    )(*args)


def shaped(*shape, dtype=F32):
    return jax.ShapeDtypeStruct(shape, dtype)


def aligned(value, unit):
    return pl.multiple_of(value * unit, unit)


def pack_body(where, trial, seabed, down, up, beside):
    for out, first in ((down, CX), (up, 0)):
        for part in range(PARTS):
            lanes = slice(part * LANE, (part + 1) * LANE)
            for member in range(MEM):
                at = 0
                for field, depth in ((1, DU), (2, DV), (0, DL)):
                    low = first - depth if first else 0
                    out[part, pl.ds(at * MEM + member, depth, stride=MEM), :] = trial[
                        member, field, low : low + depth, lanes
                    ]
                    at += depth
            low = first - DU if first else 0
            out[part, (STRIP - 1) * MEM : STRIP * MEM, :] = jnp.zeros((MEM, LANE), F32)
            out[part, (STRIP - 1) * MEM : (STRIP - 1) * MEM + DU, :] = seabed[low : low + DU, lanes]
    edge = pl.ds(pl.multiple_of(jnp.where(where[1] == 0, CY - LANE, 0), LANE), LANE)
    for member in range(MEM):
        for field in range(3):
            beside[member * 3 + field] = trial[member, field, :, edge]
    beside[MEM * 3] = seabed[:, edge]


def pack(where, trial, seabed):
    strip = shaped(PARTS, STRIP * MEM, LANE)
    return call(
        pack_body, (strip, strip, shaped(MEM * 3 + 1, CX, LANE)), (where, trial, seabed)
    )


def forecast_body(
    where, trial, seabed, above, below, beside, corner, columns, rows_of, *rest
):
    blocks, state, (level, east, north, depth) = rest[:GRP], rest[GRP], rest[GRP + 1 :]
    group, core = where[0], where[1]
    fields = (level, east, north)
    lane = lax.broadcasted_iota(jnp.int32, (1, LANE), 1)
    keep = jnp.where((lane < LANE // 2) == (core == 0), 1.0, 0.0).astype(F32)

    for field in range(3):
        for member in range(MEM):
            at = pl.ds(PAD * MEM + member, CX, stride=MEM)
            for part in range(PARTS):
                fields[field][part, at, :] = trial[
                    member, field, :, part * LANE : (part + 1) * LANE
                ]
            fields[field][PARTS, at, :] = beside[member * 3 + field] * keep
    for strip, side, top in ((above, 0, True), (below, 1, False)):
        for part in range(PARTS + 1):
            def piece(low, count):
                if part < PARTS:
                    return strip[part, low : low + count, :]
                return corner[side, low : low + count, :] * keep

            at = 0
            for ref, count in ((east, DU), (north, DV), (level, DL)):
                to = (PAD - count if top else PAD + CX) * MEM
                ref[part, to : to + count * MEM, :] = piece(at * MEM, count * MEM)
                at += count
            for row in range(DU):
                to = ((PAD - DU if top else PAD + CX) + row) * MEM
                depth[part, to : to + MEM, :] = jnp.broadcast_to(
                    piece((STRIP - 1) * MEM + row, 1), (MEM, LANE)
                )
    for row in range(CX):
        to = (PAD + row) * MEM
        for part in range(PARTS):
            depth[part, to : to + MEM, :] = jnp.broadcast_to(
                seabed[row : row + 1, part * LANE : (part + 1) * LANE], (MEM, LANE)
            )
        depth[PARTS, to : to + MEM, :] = jnp.broadcast_to(
            beside[MEM * 3, row : row + 1, :] * keep, (MEM, LANE)
        )

    wide_lane = lax.broadcasted_iota(jnp.int32, (1, WIDE), 1)
    inside = jnp.where(
        (wide_lane < CY) | ((wide_lane < CY + LANE // 2) == (core == 0)), 1.0, 0.0
    ).astype(F32)
    has_above = where[2].astype(F32)
    has_below = where[3].astype(F32)

    def get(ref, row):
        at = pl.ds(aligned(row, MEM), MEM)
        return jnp.concatenate([ref[part, at, :] for part in range(PARTS + 1)], axis=1)

    def put(ref, row, value):
        at = pl.ds(aligned(row, MEM), MEM)
        for part in range(PARTS + 1):
            ref[part, at, :] = value[:, part * LANE : (part + 1) * LANE]

    def across(value):
        return pltpu.roll(value, WIDE - 1, 1) - pltpu.roll(value, 1, 1)

    def move_level(row, carry):
        flag = jnp.where(row < PAD, has_above, jnp.where(row >= PAD + CX, has_below, 1.0))
        along = get(depth, row + 1) * get(east, row + 1) - get(depth, row - 1) * get(east, row - 1)
        spread = 0.5 * along + 0.5 * across(get(depth, row) * get(north, row))
        put(level, row, (get(level, row) - spread) * (inside * flag))
        return carry

    def move_flow(row, carry):
        slope = get(level, row + 1) - get(level, row - 1)
        put(east, row, (1.0 - FRICTION) * get(east, row) - 0.5 * slope)
        slope = across(get(level, row))
        put(north, row, (1.0 - FRICTION) * get(north, row) - 0.5 * slope)
        return carry

    for step in range(STEPS):
        reach = 2 * (STEPS - 1 - step)
        lax.fori_loop(PAD - reach - 1, PAD + CX + reach + 1, move_level, 0, unroll=2)
        lax.fori_loop(PAD - reach, PAD + CX + reach, move_flow, 0, unroll=2)

    inner = slice(PAD * MEM, (PAD + CX) * MEM)
    own = jnp.concatenate([level[part, inner, :] for part in range(PARTS)], axis=1)
    first = own.astype(BF16)
    left = own - first.astype(F32)
    second = left.astype(BF16)
    third = (left - second.astype(F32)).astype(BF16)
    pick = columns[...].astype(BF16)
    dot = functools.partial(jnp.dot, preferred_element_type=F32)
    picked = dot(first, pick) + dot(second, pick) + dot(third, pick)
    total = jnp.zeros((MEM, LANE), F32)
    for row in range(CX):
        total += picked[row * MEM : (row + 1) * MEM, :] * rows_of[row : row + 1, :]
    total = total + pltpu.roll(total, LANE // 2, 1)
    for to in range(GRP * SUB * 2):
        state[to] = total

    for other in range(GRP):
        for field in range(3):
            blocks[other][field * CX * MEM : (field + 1) * CX * MEM, :] = fields[field][
                jnp.bitwise_xor(group, other), inner, :
            ]


def forecast(where, trial, seabed, above, below, beside, corner, columns, rows_of):
    block = shaped(3 * CX * MEM, LANE)
    return call(
        forecast_body,
        (block,) * GRP + (shaped(GRP * SUB * 2, MEM, LANE),),
        (where, trial, seabed, above, below, beside, corner, columns, rows_of),
        [pltpu.VMEM((PARTS + 1, ROWS * MEM, LANE), F32)] * 4,
        flops=12_000_000,
    )


def unpack_body(where, *refs):
    blocks, out = refs[:GRP], refs[GRP]
    for other in range(GRP):
        at = pl.ds(aligned(jnp.bitwise_xor(where[0], other), LANE), LANE)
        for field in range(3):
            for member in range(MEM):
                out[member, field, :, at] = blocks[other][
                    pl.ds(field * CX * MEM + member, CX, stride=MEM), :
                ]


def unpack(where, blocks):
    return call(unpack_body, (shaped(MEM, 3, CX, CY),), (where, *blocks))[0]


def products_body(where, states, noisy, variances, masks, out):
    group = where[0]
    left, right = [], []
    for block in range(SUB * 2):
        seen = jnp.concatenate(
            [states[jnp.bitwise_xor(group, s) * (SUB * 2) + block] for s in range(GRP)], axis=0
        )
        wanted = jnp.concatenate(
            [
                noisy[block, pl.ds(aligned(jnp.bitwise_xor(group, s), MEM), MEM), :]
                for s in range(GRP)
            ],
            axis=0,
        )
        anomaly = seen - jnp.mean(seen, axis=0, keepdims=True)
        scaled = anomaly / variances[block : block + 1, :]
        left.append(
            jnp.concatenate([scaled * masks[block, r : r + 1, :] for r in range(3)], axis=0)
        )
        right.append(jnp.concatenate([anomaly, wanted - seen], axis=0))
    out[...] = lax.dot_general(
        jnp.concatenate(left, axis=1),
        jnp.concatenate(right, axis=1),
        (((1,), (1,)), ((), ())),
        precision=HIGHEST,
        preferred_element_type=F32,
    )


def region_products(where, states, noisy, variances, masks):
    return call(
        products_body, (shaped(3 * E, 2 * E),), (where, states, noisy, variances, masks)
    )[0]


def solve_body(where, own, low, high, out):
    total = own[E : 2 * E, :] + low[...] + high[...]
    row = lax.broadcasted_iota(jnp.int32, (E, 2 * E), 0)
    lane = lax.broadcasted_iota(jnp.int32, (E, 2 * E), 1)
    system = total + jnp.where(row == lane, E - 1.0, 0.0)
    for k in range(E):
        pivot = system[k : k + 1, :] / system[k : k + 1, k : k + 1]
        system = jnp.where(row == k, pivot, system - system[:, k : k + 1] * pivot)
    out[...] = system[:, E:]


def solve(where, own, low, high):
    return call(solve_body, (shaped(E, E),), (where, own, low, high))[0]


def increments_body(where, *refs):
    weights, blocks, outs = refs[0], refs[1 : 1 + GRP], refs[1 + GRP :]
    turned = weights[...].T
    coarse = turned.astype(BF16)
    fine = (turned - coarse.astype(F32)).astype(BF16)
    left = jnp.concatenate([coarse, coarse, fine], axis=1)
    group = 8

    def some(part, carry):
        pieces = []
        for inner in range(group):
            at = pl.ds(aligned(part * group + inner, MEM), MEM)
            pieces.append(jnp.concatenate([block[at, :] for block in blocks], axis=0))
        state = jnp.concatenate(pieces, axis=1)
        state = state - jnp.mean(state, axis=0, keepdims=True)
        high = state.astype(BF16)
        low = (state - high.astype(F32)).astype(BF16)
        right = jnp.concatenate([high, low, high], axis=0)
        result = jnp.dot(left, right, preferred_element_type=F32)
        for inner in range(group):
            at = pl.ds(aligned(part * group + inner, MEM), MEM)
            for other in range(GRP):
                outs[other][at, :] = result[
                    other * MEM : (other + 1) * MEM, inner * LANE : (inner + 1) * LANE
                ]
        return carry

    lax.fori_loop(0, 3 * CX // group, some, 0)


def increments(where, weights, blocks):
    return call(
        increments_body,
        (shaped(3 * CX * MEM, LANE),) * GRP,
        (where, weights, *blocks),
        flops=80_000_000,
    )


def exchange(blocks):
    return [blocks[0]] + [
        lax.ppermute(blocks[s], "grp", [(i, i ^ s) for i in range(GRP)]) for s in range(1, GRP)
    ]


def on_device(
    trial, seabed, observed, variances, perturbations, stencil_cells, stencil_weights, region_mask
):
    group, region = lax.axis_index("grp"), lax.axis_index("reg")
    sub, core = lax.axis_index("sub"), lax.axis_index("cores")
    tile = region * SUB + sub
    where = jnp.stack(
        [group, core, (tile > 0).astype(jnp.int32), (tile < REG * SUB - 1).astype(jnp.int32)]
    ).astype(jnp.int32)
    forward = [(i, i + 1) for i in range(REG * SUB - 1)]
    backward = [(i + 1, i) for i in range(REG * SUB - 1)]

    down, up, beside = pack(where, trial, seabed)
    above = lax.ppermute(down, TILE, forward)
    below = lax.ppermute(up, TILE, backward)
    beside = lax.ppermute(beside, "cores", [(0, 1), (1, 0)])

    noisy = observed[:, None] + jnp.sqrt(variances)[:, None] * perturbations
    three = lax.dynamic_slice_in_dim(
        jnp.pad(region_mask.astype(F32), ((0, 0), (1, 1))), region, 3, axis=1
    )
    known = jnp.concatenate(
        [noisy, three, variances[:, None], stencil_cells[:, :1].astype(F32), stencil_weights],
        axis=1,
    )
    fields = known.shape[1]
    known = jnp.pad(known.reshape(-1), (0, MEM * LANE - OBS * fields)).reshape(1, MEM, LANE)
    known = lax.all_to_all(
        jnp.broadcast_to(known, (GRP * SUB * 2, MEM, LANE)), SIDE, 0, 0, tiled=True
    )
    known = known.reshape(GRP, SUB * 2, MEM * LANE)[:, :, : OBS * fields]
    known = known.reshape(GRP, SUB * 2, OBS, fields).transpose(1, 3, 0, 2)
    known = known.reshape(SUB * 2, fields, GRP * OBS)
    mine = lax.dynamic_index_in_dim(known, sub * 2 + core, 0, keepdims=False)[E + 4 :]
    known = jnp.pad(known[:, : E + 4], ((0, 0), (0, 0), (0, LANE - GRP * OBS)))
    noisy, masks, scale = known[:, :E], known[:, E : E + 3], known[:, E + 3]
    scale = jnp.where(jnp.arange(LANE)[None] < GRP * OBS, scale, 1.0)
    anchor = mine[0].astype(jnp.int32)
    first_row = anchor // CY + (jnp.arange(GRP * OBS) // OBS) * (CX // GRP)
    first_column = anchor % CY
    column = jnp.arange(CY)[:, None]
    columns = jnp.concatenate(
        [column == first_column[None], column == first_column[None] + 1], axis=1
    ).astype(F32)
    row = jnp.arange(CX)[:, None]
    at_row, next_row = (row == first_row[None]).astype(F32), (row == first_row[None] + 1).astype(F32)
    rows_of = jnp.concatenate(
        [
            at_row * mine[1][None] + next_row * mine[3][None],
            at_row * mine[2][None] + next_row * mine[4][None],
        ],
        axis=1,
    )

    edge = jnp.where(core == 0, PARTS - 1, 0)
    corner = lax.ppermute(
        jnp.stack([lax.dynamic_index_in_dim(s, edge, 0, keepdims=False) for s in (above, below)]),
        "cores",
        [(0, 1), (1, 0)],
    )
    *blocks, state = forecast(
        where, trial, seabed, above, below, beside, corner, columns, rows_of
    )
    members = exchange(blocks)
    propagated_trials = unpack(where, blocks)

    states = lax.all_to_all(state, SIDE, 0, 0, tiled=True)
    products = region_products(where, states, noisy, scale, masks)
    up_region = [(i + 1, i) for i in range(REG - 1)]
    down_region = [(i, i + 1) for i in range(REG - 1)]
    from_above = lax.ppermute(products[2 * E :], "reg", down_region)
    from_below = lax.ppermute(products[:E], "reg", up_region)
    weights = solve(where, products, from_above, from_below)
    analysis_updates = unpack(where, exchange(increments(where, weights, members)))
    return (propagated_trials, analysis_updates)


def solution(mesh):
    fine = Mesh(
        mesh.devices.reshape(GRP, REG, SUB, 2), ("grp", "reg", "sub", "cores")
    )
    every = ("grp", "reg", "sub", "cores")
    state = P("grp", None, TILE, "cores")
    in_specs = (
        state,
        P(TILE, "cores"),
        P(every),
        P(every),
        P(every, None),
        P(every, None),
        P(every, None),
        P(every, None),
    )
    return jax.shard_map(
        on_device, mesh=fine, in_specs=in_specs, out_specs=(state, state), check_vma=False
    )
```

```python
import functools

import jax
import jax.numpy as jnp
from jax import lax
from jax.experimental import pallas as pl
from jax.experimental.pallas import tpu as pltpu
from jax.sharding import Mesh, PartitionSpec as P

STEPS = 3
REG = 8
GRP = 4
SUB = 4
MEM = 8
E = 32
CX = 32
CY = 512
LANE = 128
PARTS = CY // LANE
WIDE = CY + LANE
PAD = 8
OBS = 16
HALF = PAD * MEM
MIDDLE = CX * MEM - 2 * HALF
DU, DV, DL = 6, 5, 5
STRIP = DU + DV + DL + 1
FRICTION = 0.02
HIGHEST = lax.Precision.HIGHEST
F32 = jnp.float32
BF16 = jnp.bfloat16
SIDE = ("grp", "sub", "cores")
TILE = ("reg", "sub")


VMEM = pl.BlockSpec(memory_space=pltpu.VMEM)
SMEM = pl.BlockSpec(memory_space=pltpu.SMEM)


def call(body, outs, args, scratch=(), mib=16, flops=0, moved=0):
    return pl.pallas_call(
        body,
        out_shape=list(outs),
        in_specs=[SMEM] + [VMEM] * (len(args) - 1),
        out_specs=[VMEM] * len(outs),
        scratch_shapes=list(scratch),
        compiler_params=pltpu.CompilerParams(vmem_limit_bytes=mib * 1024 * 1024),
        cost_estimate=pl.CostEstimate(flops=flops, bytes_accessed=moved, transcendentals=0),
    )(*args)


def shaped(*shape, dtype=F32):
    return jax.ShapeDtypeStruct(shape, dtype)


def aligned(value, unit):
    return pl.multiple_of(value * unit, unit)


def pack_body(where, trial, seabed, down, up, beside):
    for out, first in ((down, CX), (up, 0)):
        for part in range(PARTS):
            lanes = slice(part * LANE, (part + 1) * LANE)
            for member in range(MEM):
                at = 0
                for field, depth in ((1, DU), (2, DV), (0, DL)):
                    low = first - depth if first else 0
                    out[part, pl.ds(at * MEM + member, depth, stride=MEM), :] = trial[
                        member, field, low : low + depth, lanes
                    ]
                    at += depth
            low = first - DU if first else 0
            out[part, (STRIP - 1) * MEM : STRIP * MEM, :] = jnp.zeros((MEM, LANE), F32)
            out[part, (STRIP - 1) * MEM : (STRIP - 1) * MEM + DU, :] = seabed[low : low + DU, lanes]
    edge = pl.ds(pl.multiple_of(jnp.where(where[1] == 0, CY - LANE, 0), LANE), LANE)
    for member in range(MEM):
        for field in range(3):
            beside[member * 3 + field] = trial[member, field, :, edge]
    beside[MEM * 3] = seabed[:, edge]


def pack(where, trial, seabed):
    strip = shaped(PARTS, STRIP * MEM, LANE)
    return call(
        pack_body, (strip, strip, shaped(MEM * 3 + 1, CX, LANE)), (where, trial, seabed)
    )


def row_at(row):
    return pl.ds(aligned(row, MEM), MEM)


def get(ref, row):
    at = row_at(row)
    return jnp.concatenate([ref[part, at, :] for part in range(PARTS + 1)], axis=1)


def put(ref, row, value):
    at = row_at(row)
    for part in range(PARTS + 1):
        ref[part, at, :] = value[:, part * LANE : (part + 1) * LANE]


def across(value):
    return pltpu.roll(value, WIDE - 1, 1) - pltpu.roll(value, 1, 1)


def move_level(fields, row, inside):
    level, east, north, depth = fields
    along = get(depth, row + 1) * get(east, row + 1) - get(depth, row - 1) * get(east, row - 1)
    spread = 0.5 * along + 0.5 * across(get(depth, row) * get(north, row))
    put(level, row, (get(level, row) - spread) * inside)


def move_flow(fields, row):
    level, east, north, _ = fields
    slope = get(level, row + 1) - get(level, row - 1)
    put(east, row, (1.0 - FRICTION) * get(east, row) - 0.5 * slope)
    slope = across(get(level, row))
    put(north, row, (1.0 - FRICTION) * get(north, row) - 0.5 * slope)


def kept_half(core):
    lane = lax.broadcasted_iota(jnp.int32, (1, LANE), 1)
    return jnp.where((lane < LANE // 2) == (core == 0), 1.0, 0.0).astype(F32)


def inside_of(core):
    lane = lax.broadcasted_iota(jnp.int32, (1, WIDE), 1)
    inside = (lane < CY) | ((lane < CY + LANE // 2) == (core == 0))
    return jnp.where(inside, 1.0, 0.0).astype(F32)


def inner_body(where, trial, seabed, beside, *outs):
    blocks, fields = outs[:GRP], [outs[GRP].at[f] for f in range(4)]
    keep, inside = kept_half(where[1]), inside_of(where[1])
    for field in range(3):
        for member in range(MEM):
            at = pl.ds(member, CX, stride=MEM)
            for part in range(PARTS):
                fields[field][part, at, :] = trial[
                    member, field, :, part * LANE : (part + 1) * LANE
                ]
            fields[field][PARTS, at, :] = beside[member * 3 + field] * keep
    depth = fields[3]
    for row in range(CX):
        at = slice(row * MEM, (row + 1) * MEM)
        for part in range(PARTS):
            depth[part, at, :] = jnp.broadcast_to(
                seabed[row : row + 1, part * LANE : (part + 1) * LANE], (MEM, LANE)
            )
        depth[PARTS, at, :] = jnp.broadcast_to(
            beside[MEM * 3, row : row + 1, :] * keep, (MEM, LANE)
        )

    def level_row(row, carry):
        move_level(fields, row, inside)
        return carry

    def flow_row(row, carry):
        move_flow(fields, row)
        return carry

    for step in range(STEPS):
        lax.fori_loop(2 * step + 1, CX - 2 * step - 1, level_row, 0, unroll=2)
        lax.fori_loop(2 * step + 2, CX - 2 * step - 2, flow_row, 0, unroll=2)
    for other in range(GRP):
        for field in range(3):
            blocks[other][field * MIDDLE : (field + 1) * MIDDLE, :] = fields[field][
                jnp.bitwise_xor(where[0], other), HALF : CX * MEM - HALF, :
            ]


def inner_forecast(where, trial, seabed, beside):
    fields = shaped(4, PARTS + 1, CX * MEM, LANE)
    block = shaped(3 * MIDDLE, LANE)
    return call(
        inner_body,
        (block,) * GRP + (fields,),
        (where, trial, seabed, beside),
        flops=10_000_000,
        moved=32_000_000,
    )


def sense(levels, stencils):
    anchor = stencils[0:1, :].astype(jnp.int32)
    lane = lax.broadcasted_iota(jnp.int32, (1, LANE), 1)
    of_group = (lane % (GRP * OBS)) // OBS
    row = anchor // CY + of_group * (CX // GRP)
    pick = lax.broadcasted_iota(jnp.int32, (CY, LANE), 0) == anchor % CY
    pick = jnp.where(pick, 1.0, 0.0).astype(BF16)
    first = levels.astype(BF16)
    left = levels - first.astype(F32)
    second = left.astype(BF16)
    third = (left - second.astype(F32)).astype(BF16)
    dot = functools.partial(jnp.dot, preferred_element_type=F32)
    picked = dot(first, pick) + dot(second, pick) + dot(third, pick)
    total = jnp.zeros((MEM, LANE), F32)
    for at in range(CX):
        here = jnp.where(row == at, stencils[1:2, :], 0.0)
        here += jnp.where(row + 1 == at, stencils[2:3, :], 0.0)
        total += picked[at * MEM : (at + 1) * MEM, :] * here
    return total + pltpu.roll(total, LANE // 2, 1)


def outer_body(where, inner, above, below, corner, known, *rest):
    stencils, rest = rest[:GRP], rest[GRP:]
    blocks, state, whole, scratch = rest[:GRP], rest[GRP], rest[GRP + 1], rest[GRP + 2 :]
    group, core = where[0], where[1]
    keep, inside = kept_half(core), inside_of(core)
    given = [inner.at[f] for f in range(4)]
    half = HALF
    top, bottom = scratch[:4], scratch[4:]
    for field in range(4):
        for part in range(PARTS + 1):
            top[field][part, half:, :] = given[field][part, :half, :]
            bottom[field][part, :half, :] = given[field][part, CX * MEM - half :, :]
    for strip, side, fields in ((above, 0, top), (below, 1, bottom)):
        for part in range(PARTS + 1):

            def piece(low, count):
                if part < PARTS:
                    return strip[part, low : low + count, :]
                return corner[side, low : low + count, :] * keep

            at = 0
            for field, count in ((1, DU), (2, DV), (0, DL)):
                to = half if side else (PAD - count) * MEM
                fields[field][part, to : to + count * MEM, :] = piece(at * MEM, count * MEM)
                at += count
            for row in range(DU):
                to = half + row * MEM if side else (PAD - DU + row) * MEM
                fields[3][part, to : to + MEM, :] = jnp.broadcast_to(
                    piece((STRIP - 1) * MEM + row, 1), (MEM, LANE)
                )
    has_above = inside * where[2].astype(F32)
    has_below = inside * where[3].astype(F32)
    for step in range(STEPS):
        shift = 2 * step
        for row in range(-5 + shift, 1 + shift):
            move_level(top, PAD + row, has_above if row < 0 else inside)
            move_level(bottom, PAD - 1 - row, has_below if row < 0 else inside)
        for row in range(-4 + shift, 2 + shift):
            move_flow(top, PAD + row)
            move_flow(bottom, PAD - 1 - row)

    levels = jnp.concatenate(
        [
            jnp.concatenate(
                [
                    top[0][part, half:, :],
                    given[0][part, half : CX * MEM - half, :],
                    bottom[0][part, :half, :],
                ],
                axis=0,
            )
            for part in range(PARTS)
        ],
        axis=1,
    )
    total = sense(levels, sum(s[...] for s in stencils))
    for to in range(GRP * SUB * 2):
        state[to, :MEM, :] = total
        state[to, MEM:, :] = known[...]

    for field in range(3):
        for part in range(PARTS):
            whole[field, part, :half, :] = top[field][part, half:, :]
            whole[field, part, half:, :] = bottom[field][part, :half, :]
        for other in range(GRP):
            blocks[other][field * MIDDLE : (field + 1) * MIDDLE, :] = whole[
                field, jnp.bitwise_xor(group, other)
            ]


def outer_forecast(where, inner, above, below, corner, known, stencils):
    block = shaped(3 * MIDDLE, LANE)
    return call(
        outer_body,
        (block,) * GRP
        + (shaped(GRP * SUB * 2, 2 * MEM, LANE), shaped(3, PARTS, 2 * HALF, LANE)),
        (where, inner, above, below, corner, known, *stencils),
        [pltpu.VMEM((PARTS + 1, 2 * PAD * MEM, LANE), F32)] * 8,
    )


def unpack_body(where, *refs):
    blocks, out = refs[:GRP], refs[GRP]
    for other in range(GRP):
        at = pl.ds(aligned(jnp.bitwise_xor(where[0], other), LANE), LANE)
        for field in range(3):
            for member in range(MEM):
                out[member, field, :, at] = blocks[other][
                    pl.ds(field * CX * MEM + member, CX, stride=MEM), :
                ]


def unpack(where, blocks):
    return call(unpack_body, (shaped(MEM, 3, CX, CY),), (where, *blocks))[0]


def spread_out_body(where, inner, outer, out):
    for part in range(PARTS):
        lanes = slice(part * LANE, (part + 1) * LANE)
        for field in range(3):
            for member in range(MEM):
                out[member, field, PAD : CX - PAD, lanes] = inner[
                    field, part, pl.ds(HALF + member, CX - 2 * PAD, stride=MEM), :
                ]
                out[member, field, :PAD, lanes] = outer[
                    field, part, pl.ds(member, PAD, stride=MEM), :
                ]
                out[member, field, CX - PAD :, lanes] = outer[
                    field, part, pl.ds(HALF + member, PAD, stride=MEM), :
                ]


def spread_out(where, inner, outer):
    return call(spread_out_body, (shaped(MEM, 3, CX, CY),), (where, inner, outer))[0]


def products_body(where, states, out, wanted_at):
    group = where[0]
    lane = lax.broadcasted_iota(jnp.int32, (1, LANE), 1)
    left, right = [], []
    for block in range(SUB * 2):
        noisy, other = [jnp.zeros((MEM, LANE), F32)] * GRP, jnp.zeros((MEM, LANE), F32)
        for source in range(GRP):
            held = states[source * (SUB * 2) + block, MEM:, :]
            here = lane // OBS == source
            for part in range(GRP):
                turned = pltpu.roll(held, (source - part) * OBS % LANE, 1)
                noisy[part] = jnp.where(here, turned, noisy[part])
            turned = pltpu.roll(held, (source - GRP) * OBS % LANE, 1)
            other = jnp.where(here, turned, other)
        for part in range(GRP):
            wanted_at[block, part] = noisy[part]
        seen = jnp.concatenate(
            [
                states[jnp.bitwise_xor(group, s) * (SUB * 2) + block, :MEM, :]
                for s in range(GRP)
            ],
            axis=0,
        )
        wanted = jnp.concatenate(
            [wanted_at[block, jnp.bitwise_xor(group, s)] for s in range(GRP)], axis=0
        )
        anomaly = seen - jnp.mean(seen, axis=0, keepdims=True)
        scaled = anomaly / jnp.where(lane < GRP * OBS, other[3:4, :], 1.0)
        left.append(jnp.concatenate([scaled * other[r : r + 1, :] for r in range(3)], axis=0))
        right.append(jnp.concatenate([anomaly, wanted - seen], axis=0))
    out[...] = lax.dot_general(
        jnp.concatenate(left, axis=1),
        jnp.concatenate(right, axis=1),
        (((1,), (1,)), ((), ())),
        precision=HIGHEST,
        preferred_element_type=F32,
    )


def region_products(where, states):
    return call(
        products_body,
        (shaped(3 * E, 2 * E),),
        (where, states),
        [pltpu.VMEM((SUB * 2, GRP, MEM, LANE), F32)],
    )[0]


def solve_body(where, own, low, high, out):
    total = own[E : 2 * E, :] + low[...] + high[...]
    row = lax.broadcasted_iota(jnp.int32, (E, 2 * E), 0)
    lane = lax.broadcasted_iota(jnp.int32, (E, 2 * E), 1)
    system = total + jnp.where(row == lane, E - 1.0, 0.0)
    for k in range(E):
        pivot = system[k : k + 1, :] / system[k : k + 1, k : k + 1]
        system = jnp.where(row == k, pivot, system - system[:, k : k + 1] * pivot)
    out[...] = system[:, E:]


def solve(where, own, low, high):
    return call(solve_body, (shaped(E, E),), (where, own, low, high))[0]


def increments_body(where, *refs):
    weights, middle, edge, outs = refs[0], refs[1 : 1 + GRP], refs[1 + GRP : 1 + 2 * GRP], refs[1 + 2 * GRP :]
    turned = weights[...].T
    coarse = turned.astype(BF16)
    fine = (turned - coarse.astype(F32)).astype(BF16)
    left = jnp.concatenate([coarse, coarse, fine], axis=1)

    def some(blocks, low, to):
        pieces = []
        for row in range(PAD):
            at = slice(low + row * MEM, low + (row + 1) * MEM)
            pieces.append(jnp.concatenate([block[at, :] for block in blocks], axis=0))
        state = jnp.concatenate(pieces, axis=1)
        state = state - jnp.mean(state, axis=0, keepdims=True)
        high = state.astype(BF16)
        low_part = (state - high.astype(F32)).astype(BF16)
        right = jnp.concatenate([high, low_part, high], axis=0)
        result = jnp.dot(left, right, preferred_element_type=F32)
        for row in range(PAD):
            for other in range(GRP):
                outs[other][to + row * MEM : to + (row + 1) * MEM, :] = result[
                    other * MEM : (other + 1) * MEM, row * LANE : (row + 1) * LANE
                ]

    for field in range(3):
        at, to = field * MIDDLE, field * CX * MEM
        some(edge, at, to)
        some(middle, at, to + HALF)
        some(middle, at + HALF, to + 2 * HALF)
        some(edge, at + HALF, to + 3 * HALF)


def increments(where, weights, middle, edge):
    return call(
        increments_body,
        (shaped(3 * CX * MEM, LANE),) * GRP,
        (where, weights, *middle, *edge),
    )


def exchange(blocks):
    return [blocks[0]] + [
        lax.ppermute(blocks[s], "grp", [(i, i ^ s) for i in range(GRP)]) for s in range(1, GRP)
    ]


def on_device(
    trial, seabed, observed, variances, perturbations, stencil_cells, stencil_weights, region_mask
):
    group, region = lax.axis_index("grp"), lax.axis_index("reg")
    sub, core = lax.axis_index("sub"), lax.axis_index("cores")
    tile = region * SUB + sub
    where = jnp.stack(
        [group, core, (tile > 0).astype(jnp.int32), (tile < REG * SUB - 1).astype(jnp.int32)]
    ).astype(jnp.int32)
    forward = [(i, i + 1) for i in range(REG * SUB - 1)]
    backward = [(i + 1, i) for i in range(REG * SUB - 1)]

    down, up, beside = pack(where, trial, seabed)
    above = lax.ppermute(down, TILE, forward)
    below = lax.ppermute(up, TILE, backward)
    beside = lax.ppermute(beside, "cores", [(0, 1), (1, 0)])

    count, wide = GRP * OBS, LANE // 2
    anchor = stencil_cells[:, 0].astype(F32)
    pair = jnp.stack([anchor, anchor + 1.0])
    uses = stencil_weights.T
    stencil = jnp.stack([pair, uses[:2], uses[2:]])
    slot = (jnp.arange(GRP) == group).astype(F32)
    stencil = (stencil[:, :, None, :] * slot[None, None, :, None]).reshape(3, 2 * count)
    stencil = jnp.pad(stencil, ((0, MEM - 3), (0, 0)))
    noisy = observed[:, None] + jnp.sqrt(variances)[:, None] * perturbations
    noisy = noisy.T.reshape(GRP, MEM, OBS).transpose(1, 0, 2).reshape(MEM, count)
    three = lax.dynamic_slice_in_dim(
        jnp.pad(region_mask.astype(F32), ((0, 0), (1, 1))), region, 3, axis=1
    )
    three = jnp.concatenate([three.T, variances[None]], axis=0)
    known = jnp.concatenate(
        [noisy, jnp.pad(three, ((0, MEM - 4), (0, wide - OBS)))], axis=1
    )

    *middle, inner = inner_forecast(where, trial, seabed, beside)
    stencil, inner = lax.optimization_barrier((stencil, inner))
    stencils = exchange([stencil] * GRP)
    above, below, _ = lax.optimization_barrier((above, below, stencils[1:]))
    edge = jnp.where(core == 0, PARTS - 1, 0)

    def outer_rows(above, below, inner, known, stencils):
        ends = [lax.dynamic_index_in_dim(s, edge, 0, keepdims=False) for s in (above, below)]
        corner = lax.ppermute(jnp.stack(ends), "cores", [(0, 1), (1, 0)])
        *outer, state, rest = outer_forecast(where, inner, above, below, corner, known, stencils)
        return outer, rest, lax.all_to_all(state, SIDE, 0, 0, tiled=True)

    def nothing(*args):
        block = jnp.zeros((3 * MIDDLE, LANE), F32)
        rest = jnp.zeros((3, PARTS, 2 * HALF, LANE), F32)
        return [block] * GRP, rest, jnp.zeros((GRP * SUB * 2, 2 * MEM, LANE), F32)

    middle, *_ = lax.optimization_barrier((middle, stencils[1:]))
    middle = exchange(middle)
    outer, rest, states = lax.cond(
        group < GRP, outer_rows, nothing, above, below, inner, known, stencils
    )
    outer = exchange(outer)
    propagated_trials = spread_out(where, inner, rest)

    up_region = [(i + 1, i) for i in range(REG - 1)]
    down_region = [(i, i + 1) for i in range(REG - 1)]
    products = region_products(where, states)
    products, _ = lax.optimization_barrier((products, middle[1:]))
    from_above = lax.ppermute(products[2 * E :], "reg", down_region)
    from_below = lax.ppermute(products[:E], "reg", up_region)
    weights = solve(where, products, from_above, from_below)
    analysis_updates = unpack(where, exchange(increments(where, weights, middle, outer)))
    return (propagated_trials, analysis_updates)


def solution(mesh):
    fine = Mesh(
        mesh.devices.reshape(GRP, REG, SUB, 2), ("grp", "reg", "sub", "cores")
    )
    every = ("grp", "reg", "sub", "cores")
    state = P("grp", None, TILE, "cores")
    in_specs = (
        state,
        P(TILE, "cores"),
        P(every),
        P(every),
        P(every, None),
        P(every, None),
        P(every, None),
        P(every, None),
    )
    return jax.shard_map(
        on_device, mesh=fine, in_specs=in_specs, out_specs=(state, state), check_vma=False
    )
```

```python
import functools

import jax
import jax.numpy as jnp
from jax import lax
from jax.experimental import pallas as pl
from jax.experimental.pallas import tpu as pltpu
from jax.sharding import Mesh, PartitionSpec as P

STEPS = 3
REG = 8
GRP = 4
SUB = 4
MEM = 8
E = 32
CX = 32
CY = 512
LANE = 128
PARTS = CY // LANE
WIDE = CY + LANE
PAD = 8
OBS = 16
HALF = PAD * MEM
MIDDLE = CX * MEM - 2 * HALF
DU, DV, DL = 6, 5, 5
STRIP = DU + DV + DL + 1
FRICTION = 0.02
HIGHEST = lax.Precision.HIGHEST
F32 = jnp.float32
BF16 = jnp.bfloat16
SIDE = ("grp", "sub", "cores")
TILE = ("reg", "sub")


VMEM = pl.BlockSpec(memory_space=pltpu.VMEM)
SMEM = pl.BlockSpec(memory_space=pltpu.SMEM)
ANY = pl.BlockSpec(memory_space=pl.ANY)


def call(body, outs, args, scratch=(), mib=16, flops=0, moved=0):
    return pl.pallas_call(
        body,
        out_shape=list(outs),
        in_specs=[SMEM] + [VMEM] * (len(args) - 1),
        out_specs=[VMEM] * len(outs),
        scratch_shapes=list(scratch),
        compiler_params=pltpu.CompilerParams(vmem_limit_bytes=mib * 1024 * 1024),
        cost_estimate=pl.CostEstimate(flops=flops, bytes_accessed=moved, transcendentals=0),
    )(*args)


def shaped(*shape, dtype=F32):
    return jax.ShapeDtypeStruct(shape, dtype)


def aligned(value, unit):
    return pl.multiple_of(value * unit, unit)


def pack_body(where, trial, seabed, down, up, beside, last, first, bed, strips, edges, sems):
    edge = pl.ds(pl.multiple_of(jnp.where(where[1] == 0, CY - LANE, 0), LANE), LANE)
    moves = [
        (trial.at[:, :, CX - PAD :, :], last),
        (seabed, bed),
        (trial.at[:, :, :PAD, :], first),
        (trial.at[:, :, :, edge], edges.at[:MEM]),
        (strips.at[0], down),
        (strips.at[1], up),
        (edges, beside),
    ]
    copies = [pltpu.make_async_copy(*move, sems.at[i]) for i, move in enumerate(moves)]
    for copy in copies[:4]:
        copy.start()
    for side, (rows, end) in enumerate(((last, True), (first, False))):
        if end:
            copies[0].wait()
            copies[1].wait()
        else:
            copies[2].wait()
        for part in range(PARTS):
            lanes = slice(part * LANE, (part + 1) * LANE)
            for member in range(MEM):
                at = 0
                for field, depth in ((1, DU), (2, DV), (0, DL)):
                    low = PAD - depth if end else 0
                    strips[side, part, pl.ds(at * MEM + member, depth, stride=MEM), :] = rows[
                        member, field, low : low + depth, lanes
                    ]
                    at += depth
            low, to = CX - DU if end else 0, (STRIP - 1) * MEM
            strips[side, part, to : to + MEM, :] = jnp.zeros((MEM, LANE), F32)
            strips[side, part, to : to + DU, :] = bed[low : low + DU, lanes]
        copies[4 + side].start()
    for same in range(3):
        edges[MEM, same] = bed[:, edge]
    copies[3].wait()
    for copy in copies[6:]:
        copy.start()
    for copy in copies[4:]:
        copy.wait()


def pack(where, trial, seabed):
    strip = shaped(PARTS, STRIP * MEM, LANE)
    rows = pltpu.VMEM((MEM, 3, PAD, CY), F32)
    return pl.pallas_call(
        pack_body,
        out_shape=[strip, strip, shaped(MEM + 1, 3, CX, LANE)],
        in_specs=[SMEM, ANY, ANY],
        out_specs=[ANY] * 3,
        scratch_shapes=[
            rows,
            rows,
            pltpu.VMEM((CX, CY), F32),
            pltpu.VMEM((2,) + strip.shape, F32),
            pltpu.VMEM((MEM + 1, 3, CX, LANE), F32),
            pltpu.SemaphoreType.DMA((7,)),
        ],
        compiler_params=pltpu.CompilerParams(vmem_limit_bytes=60 * 1024 * 1024),
    )(where, trial, seabed)


def row_at(row):
    return pl.ds(aligned(row, MEM), MEM)


def get(ref, row):
    at = row_at(row)
    return jnp.concatenate([ref[part, at, :] for part in range(PARTS + 1)], axis=1)


def put(ref, row, value):
    at = row_at(row)
    for part in range(PARTS + 1):
        ref[part, at, :] = value[:, part * LANE : (part + 1) * LANE]


def across(value):
    return pltpu.roll(value, WIDE - 1, 1) - pltpu.roll(value, 1, 1)


def move_level(fields, row, inside):
    level, east, north, depth = fields
    along = get(depth, row + 1) * get(east, row + 1) - get(depth, row - 1) * get(east, row - 1)
    spread = 0.5 * along + 0.5 * across(get(depth, row) * get(north, row))
    put(level, row, (get(level, row) - spread) * inside)


def move_flow(fields, row):
    level, east, north, _ = fields
    slope = get(level, row + 1) - get(level, row - 1)
    put(east, row, (1.0 - FRICTION) * get(east, row) - 0.5 * slope)
    slope = across(get(level, row))
    put(north, row, (1.0 - FRICTION) * get(north, row) - 0.5 * slope)


def kept_half(core):
    lane = lax.broadcasted_iota(jnp.int32, (1, LANE), 1)
    return jnp.where((lane < LANE // 2) == (core == 0), 1.0, 0.0).astype(F32)


def inside_of(core):
    lane = lax.broadcasted_iota(jnp.int32, (1, WIDE), 1)
    inside = (lane < CY) | ((lane < CY + LANE // 2) == (core == 0))
    return jnp.where(inside, 1.0, 0.0).astype(F32)


def inner_body(where, trial, seabed, beside, *outs):
    blocks, fields = outs[:GRP], [outs[GRP].at[f] for f in range(4)]
    keep, inside = kept_half(where[1]), inside_of(where[1])
    for field in range(3):
        for member in range(MEM):
            at = pl.ds(member, CX, stride=MEM)
            for part in range(PARTS):
                fields[field][part, at, :] = trial[
                    member, field, :, part * LANE : (part + 1) * LANE
                ]
            fields[field][PARTS, at, :] = beside[member, field] * keep
    depth = fields[3]
    for row in range(CX):
        at = slice(row * MEM, (row + 1) * MEM)
        for part in range(PARTS):
            depth[part, at, :] = jnp.broadcast_to(
                seabed[row : row + 1, part * LANE : (part + 1) * LANE], (MEM, LANE)
            )
        depth[PARTS, at, :] = jnp.broadcast_to(
            beside[MEM, 0, row : row + 1, :] * keep, (MEM, LANE)
        )

    def level_row(row, carry):
        move_level(fields, row, inside)
        return carry

    def flow_row(row, carry):
        move_flow(fields, row)
        return carry

    for step in range(STEPS):
        lax.fori_loop(2 * step + 1, CX - 2 * step - 1, level_row, 0, unroll=2)
        lax.fori_loop(2 * step + 2, CX - 2 * step - 2, flow_row, 0, unroll=2)
    for other in range(GRP):
        for field in range(3):
            blocks[other][field * MIDDLE : (field + 1) * MIDDLE, :] = fields[field][
                jnp.bitwise_xor(where[0], other), HALF : CX * MEM - HALF, :
            ]


def inner_forecast(where, trial, seabed, beside):
    fields = shaped(4, PARTS + 1, CX * MEM, LANE)
    block = shaped(3 * MIDDLE, LANE)
    return call(
        inner_body,
        (block,) * GRP + (fields,),
        (where, trial, seabed, beside),
        flops=10_000_000,
        moved=32_000_000,
    )


def sense(levels, stencils):
    anchor = stencils[0:1, :].astype(jnp.int32)
    lane = lax.broadcasted_iota(jnp.int32, (1, LANE), 1)
    of_group = (lane % (GRP * OBS)) // OBS
    row = anchor // CY + of_group * (CX // GRP)
    pick = lax.broadcasted_iota(jnp.int32, (CY, LANE), 0) == anchor % CY
    pick = jnp.where(pick, 1.0, 0.0).astype(BF16)
    first = levels.astype(BF16)
    left = levels - first.astype(F32)
    second = left.astype(BF16)
    third = (left - second.astype(F32)).astype(BF16)
    dot = functools.partial(jnp.dot, preferred_element_type=F32)
    picked = dot(first, pick) + dot(second, pick) + dot(third, pick)
    total = jnp.zeros((MEM, LANE), F32)
    for at in range(CX):
        here = jnp.where(row == at, stencils[1:2, :], 0.0)
        here += jnp.where(row + 1 == at, stencils[2:3, :], 0.0)
        total += picked[at * MEM : (at + 1) * MEM, :] * here
    return total + pltpu.roll(total, LANE // 2, 1)


def outer_body(where, inner, above, below, corner, known, *rest):
    stencils, rest = rest[:GRP], rest[GRP:]
    blocks, state, whole, scratch = rest[:GRP], rest[GRP], rest[GRP + 1], rest[GRP + 2 :]
    group, core = where[0], where[1]
    keep, inside = kept_half(core), inside_of(core)
    given = [inner.at[f] for f in range(4)]
    half = HALF
    top, bottom = scratch[:4], scratch[4:]
    for field in range(4):
        for part in range(PARTS + 1):
            top[field][part, half:, :] = given[field][part, :half, :]
            bottom[field][part, :half, :] = given[field][part, CX * MEM - half :, :]
    for strip, side, fields in ((above, 0, top), (below, 1, bottom)):
        for part in range(PARTS + 1):

            def piece(low, count):
                if part < PARTS:
                    return strip[part, low : low + count, :]
                return corner[side, low : low + count, :] * keep

            at = 0
            for field, count in ((1, DU), (2, DV), (0, DL)):
                to = half if side else (PAD - count) * MEM
                fields[field][part, to : to + count * MEM, :] = piece(at * MEM, count * MEM)
                at += count
            for row in range(DU):
                to = half + row * MEM if side else (PAD - DU + row) * MEM
                fields[3][part, to : to + MEM, :] = jnp.broadcast_to(
                    piece((STRIP - 1) * MEM + row, 1), (MEM, LANE)
                )
    has_above = inside * where[2].astype(F32)
    has_below = inside * where[3].astype(F32)
    for step in range(STEPS):
        shift = 2 * step
        for row in range(-5 + shift, 1 + shift):
            move_level(top, PAD + row, has_above if row < 0 else inside)
            move_level(bottom, PAD - 1 - row, has_below if row < 0 else inside)
        for row in range(-4 + shift, 2 + shift):
            move_flow(top, PAD + row)
            move_flow(bottom, PAD - 1 - row)

    levels = jnp.concatenate(
        [
            jnp.concatenate(
                [
                    top[0][part, half:, :],
                    given[0][part, half : CX * MEM - half, :],
                    bottom[0][part, :half, :],
                ],
                axis=0,
            )
            for part in range(PARTS)
        ],
        axis=1,
    )
    total = sense(levels, sum(s[...] for s in stencils))
    lane = lax.broadcasted_iota(jnp.int32, (1, LANE), 1)
    total = jnp.where(lane < GRP * OBS, total[: MEM // 2, :], total[MEM // 2 :, :])
    for to in range(GRP * SUB * 2):
        state[3 * to] = total
        state[3 * to + 1] = known[0]
        state[3 * to + 2] = known[1]

    for field in range(3):
        for part in range(PARTS):
            whole[field, part, :half, :] = top[field][part, half:, :]
            whole[field, part, half:, :] = bottom[field][part, :half, :]
        for other in range(GRP):
            blocks[other][field * MIDDLE : (field + 1) * MIDDLE, :] = whole[
                field, jnp.bitwise_xor(group, other)
            ]


def outer_forecast(where, inner, strips, known, stencils):
    block = shaped(3 * MIDDLE, LANE)
    return call(
        outer_body,
        (block,) * GRP
        + (shaped(3 * GRP * SUB * 2, MEM // 2, LANE), shaped(3, PARTS, 2 * HALF, LANE)),
        (where, inner, *strips, known, *stencils),
        [pltpu.VMEM((PARTS + 1, 2 * PAD * MEM, LANE), F32)] * 8,
    )


def turned_rows(block, field, member):
    return block[pl.ds(field * CX * MEM + member, CX, stride=MEM), :]


def unpack_body(where, *refs):
    blocks, out = refs[:-1], refs[-1]
    for other, block in enumerate(blocks):
        at = pl.ds(aligned(jnp.bitwise_xor(where[0], other), LANE), LANE)
        for field in range(3):
            for member in range(MEM):
                out[member, field, :, at] = turned_rows(block, field, member)


def unpack_last_body(where, block, _, out, held, sem):
    for field in range(3):
        for member in range(MEM):
            held[member, field] = turned_rows(block, field, member)
    at = pl.ds(aligned(jnp.bitwise_xor(where[0], GRP - 1), LANE), LANE)
    copy = pltpu.make_async_copy(held, out.at[:, :, :, at], sem)
    copy.start()
    copy.wait()


def unpack(where, blocks):
    out = shaped(MEM, 3, CX, CY)
    early = call(unpack_body, (out,), (where, *blocks[:-1]))[0]
    return pl.pallas_call(
        unpack_last_body,
        out_shape=out,
        in_specs=[SMEM, VMEM, ANY],
        out_specs=ANY,
        scratch_shapes=[pltpu.VMEM((MEM, 3, CX, LANE), F32), pltpu.SemaphoreType.DMA],
        input_output_aliases={2: 0},
        compiler_params=pltpu.CompilerParams(vmem_limit_bytes=16 * 1024 * 1024),
    )(where, blocks[-1], early)


def spread_out_body(where, inner, outer, out):
    for part in range(PARTS):
        lanes = slice(part * LANE, (part + 1) * LANE)
        for field in range(3):
            for member in range(MEM):
                out[member, field, PAD : CX - PAD, lanes] = inner[
                    field, part, pl.ds(HALF + member, CX - 2 * PAD, stride=MEM), :
                ]
                out[member, field, :PAD, lanes] = outer[
                    field, part, pl.ds(member, PAD, stride=MEM), :
                ]
                out[member, field, CX - PAD :, lanes] = outer[
                    field, part, pl.ds(HALF + member, PAD, stride=MEM), :
                ]


def spread_out(where, inner, outer):
    return call(spread_out_body, (shaped(MEM, 3, CX, CY),), (where, inner, outer))[0]


def products_body(where, states, out, wanted_at):
    group = where[0]
    lane = lax.broadcasted_iota(jnp.int32, (1, LANE), 1)

    def unfolded(at):
        value = states[at]
        return jnp.concatenate([value, pltpu.roll(value, LANE // 2, 1)], axis=0)

    left, right = [], []
    for block in range(SUB * 2):
        noisy = [jnp.zeros((MEM, LANE), F32)] * GRP
        other = jnp.zeros((MEM // 2, LANE), F32)
        for source in range(GRP):
            at = 3 * (source * (SUB * 2) + block)
            held, here = unfolded(at + 1), lane // OBS == source
            for part in range(GRP):
                turned = pltpu.roll(held, (source - part) * OBS % LANE, 1)
                noisy[part] = jnp.where(here, turned, noisy[part])
            other = jnp.where(here, pltpu.roll(states[at + 2], source * OBS, 1), other)
        for part in range(GRP):
            wanted_at[block, part] = noisy[part]
        seen = jnp.concatenate(
            [
                unfolded(3 * (jnp.bitwise_xor(group, s) * (SUB * 2) + block))
                for s in range(GRP)
            ],
            axis=0,
        )
        wanted = jnp.concatenate(
            [wanted_at[block, jnp.bitwise_xor(group, s)] for s in range(GRP)], axis=0
        )
        anomaly = seen - jnp.mean(seen, axis=0, keepdims=True)
        scaled = anomaly / jnp.where(lane < GRP * OBS, other[3:4, :], 1.0)
        left.append(jnp.concatenate([scaled * other[r : r + 1, :] for r in range(3)], axis=0))
        right.append(jnp.concatenate([anomaly, wanted - seen], axis=0))
    out[...] = lax.dot_general(
        jnp.concatenate(left, axis=1),
        jnp.concatenate(right, axis=1),
        (((1,), (1,)), ((), ())),
        precision=HIGHEST,
        preferred_element_type=F32,
    )


def region_products(where, states):
    return call(
        products_body,
        (shaped(3 * E, 2 * E),),
        (where, states),
        [pltpu.VMEM((SUB * 2, GRP, MEM, LANE), F32)],
    )[0]


def solve_body(where, own, low, high, out):
    total = own[E : 2 * E, :] + low[...] + high[...]
    row = lax.broadcasted_iota(jnp.int32, (E, 2 * E), 0)
    lane = lax.broadcasted_iota(jnp.int32, (E, 2 * E), 1)
    system = total + jnp.where(row == lane, E - 1.0, 0.0)
    for k in range(E):
        pivot = system[k : k + 1, :] / system[k : k + 1, k : k + 1]
        system = jnp.where(row == k, pivot, system - system[:, k : k + 1] * pivot)
    out[...] = system[:, E:]


def solve(where, own, low, high):
    return call(solve_body, (shaped(E, E),), (where, own, low, high))[0]


def increments_body(where, *refs):
    weights, middle, edge, outs = refs[0], refs[1 : 1 + GRP], refs[1 + GRP : 1 + 2 * GRP], refs[1 + 2 * GRP :]
    turned = weights[...].T
    coarse = turned.astype(BF16)
    fine = (turned - coarse.astype(F32)).astype(BF16)
    left = jnp.concatenate([coarse, coarse, fine], axis=1)

    def some(blocks, low, to):
        pieces = []
        for row in range(PAD):
            at = slice(low + row * MEM, low + (row + 1) * MEM)
            pieces.append(jnp.concatenate([block[at, :] for block in blocks], axis=0))
        state = jnp.concatenate(pieces, axis=1)
        state = state - jnp.mean(state, axis=0, keepdims=True)
        high = state.astype(BF16)
        low_part = (state - high.astype(F32)).astype(BF16)
        right = jnp.concatenate([high, low_part, high], axis=0)
        result = jnp.dot(left, right, preferred_element_type=F32)
        for row in range(PAD):
            for other in range(GRP):
                outs[other][to + row * MEM : to + (row + 1) * MEM, :] = result[
                    other * MEM : (other + 1) * MEM, row * LANE : (row + 1) * LANE
                ]

    for field in range(3):
        at, to = field * MIDDLE, field * CX * MEM
        some(edge, at, to)
        some(middle, at, to + HALF)
        some(middle, at + HALF, to + 2 * HALF)
        some(edge, at + HALF, to + 3 * HALF)


def increments(where, weights, middle, edge):
    return call(
        increments_body,
        (shaped(3 * CX * MEM, LANE),) * GRP,
        (where, weights, *middle, *edge),
    )


def exchange(blocks):
    return [blocks[0]] + [
        lax.ppermute(blocks[s], "grp", [(i, i ^ s) for i in range(GRP)]) for s in range(1, GRP)
    ]


def on_device(
    trial, seabed, observed, variances, perturbations, stencil_cells, stencil_weights, region_mask
):
    group, region = lax.axis_index("grp"), lax.axis_index("reg")
    sub, core = lax.axis_index("sub"), lax.axis_index("cores")
    tile = region * SUB + sub
    where = jnp.stack(
        [group, core, (tile > 0).astype(jnp.int32), (tile < REG * SUB - 1).astype(jnp.int32)]
    ).astype(jnp.int32)
    forward = [(i, i + 1) for i in range(REG * SUB - 1)]
    backward = [(i + 1, i) for i in range(REG * SUB - 1)]

    down, up, beside = pack(where, trial, seabed)
    above = lax.ppermute(down, TILE, forward)
    below = lax.ppermute(up, TILE, backward)
    beside = lax.ppermute(beside, "cores", [(0, 1), (1, 0)])

    count = GRP * OBS
    anchor = stencil_cells[:, 0].astype(F32)
    pair = jnp.stack([anchor, anchor + 1.0])
    uses = stencil_weights.T
    stencil = jnp.stack([pair, uses[:2], uses[2:]])
    slot = (jnp.arange(GRP) == group).astype(F32)
    stencil = (stencil[:, :, None, :] * slot[None, None, :, None]).reshape(3, 2 * count)
    stencil = jnp.pad(stencil, ((0, MEM - 3), (0, 0)))
    noisy = observed[:, None] + jnp.sqrt(variances)[:, None] * perturbations
    noisy = noisy.T.reshape(GRP, 2, MEM // 2, OBS).transpose(2, 1, 0, 3).reshape(MEM // 2, LANE)
    three = lax.dynamic_slice_in_dim(
        jnp.pad(region_mask.astype(F32), ((0, 0), (1, 1))), region, 3, axis=1
    )
    three = jnp.concatenate([three.T, variances[None]], axis=0)
    known = jnp.stack([noisy, jnp.pad(three, ((0, 0), (0, LANE - OBS)))])

    stencil, beside = lax.optimization_barrier((stencil, beside))
    stencils = exchange([stencil] * GRP)
    *middle, inner = inner_forecast(where, trial, seabed, beside)
    above, below, _ = lax.optimization_barrier((above, below, stencils[1:]))

    def outer_rows(above, below, inner, known, stencils):
        edge = jnp.where(core == 0, PARTS - 1, 0)
        ends = [lax.dynamic_index_in_dim(s, edge, 0, keepdims=False) for s in (above, below)]
        corner = lax.ppermute(jnp.stack(ends), "cores", [(0, 1), (1, 0)])
        *outer, state, rest = outer_forecast(
            where, inner, (above, below, corner), known, stencils
        )
        return outer, rest, lax.all_to_all(state, SIDE, 0, 0, tiled=True)

    def nothing(*args):
        block = jnp.zeros((3 * MIDDLE, LANE), F32)
        rest = jnp.zeros((3, PARTS, 2 * HALF, LANE), F32)
        return [block] * GRP, rest, jnp.zeros((3 * GRP * SUB * 2, MEM // 2, LANE), F32)

    middle, *_ = lax.optimization_barrier((middle, stencils[1:]))
    middle = exchange(middle)
    outer, rest, states = lax.cond(
        group < GRP, outer_rows, nothing, above, below, inner, known, stencils
    )
    outer = exchange(outer)
    propagated_trials = spread_out(where, inner, rest)

    pairs = [
        (r * SUB + q, (r + 1) * SUB + (q ^ 2)) for r in range(REG - 1) for q in range(SUB)
    ]
    products = region_products(where, states)
    products, _ = lax.optimization_barrier((products, middle[1:]))
    from_above = lax.ppermute(products[2 * E :], TILE, pairs)
    from_below = lax.ppermute(products[:E], TILE, [(b, a) for a, b in pairs])
    weights = solve(where, products, from_above, from_below)
    analysis_updates = unpack(where, exchange(increments(where, weights, middle, outer)))
    return (propagated_trials, analysis_updates)


def solution(mesh):
    fine = Mesh(
        mesh.devices.reshape(GRP, REG, SUB, 2), ("grp", "reg", "sub", "cores")
    )
    every = ("grp", "reg", "sub", "cores")
    state = P("grp", None, TILE, "cores")
    in_specs = (
        state,
        P(TILE, "cores"),
        P(every),
        P(every),
        P(every, None),
        P(every, None),
        P(every, None),
        P(every, None),
    )
    return jax.shard_map(
        on_device, mesh=fine, in_specs=in_specs, out_specs=(state, state), check_vma=False
    )
```

```python
import functools

import jax
import jax.numpy as jnp
from jax import lax
from jax.experimental import pallas as pl
from jax.experimental.pallas import tpu as pltpu
from jax.sharding import Mesh, PartitionSpec as P

STEPS = 3
REG = 8
GRP = 4
SUB = 4
MEM = 8
E = 32
CX = 32
CY = 512
LANE = 128
PARTS = CY // LANE
WIDE = CY + LANE
PAD = 8
OBS = 16
HALF = PAD * MEM
MIDDLE = CX * MEM - 2 * HALF
DU, DV, DL = 4, 5, 5
STRIP = DU + DV + DL + 1
FRICTION = 0.02
HIGHEST = lax.Precision.HIGHEST
EARLY, LATE = (0, 1, 3), 2
F32 = jnp.float32
BF16 = jnp.bfloat16
SIDE = ("grp", "sub", "cores")
TILE = ("reg", "sub")


VMEM = pl.BlockSpec(memory_space=pltpu.VMEM)
SMEM = pl.BlockSpec(memory_space=pltpu.SMEM)
ANY = pl.BlockSpec(memory_space=pl.ANY)


def call(body, outs, args, scratch=(), mib=16, flops=0, moved=0):
    return pl.pallas_call(
        body,
        out_shape=list(outs),
        in_specs=[SMEM] + [VMEM] * (len(args) - 1),
        out_specs=[VMEM] * len(outs),
        scratch_shapes=list(scratch),
        compiler_params=pltpu.CompilerParams(vmem_limit_bytes=mib * 1024 * 1024),
        cost_estimate=pl.CostEstimate(flops=flops, bytes_accessed=moved, transcendentals=0),
    )(*args)


def shaped(*shape, dtype=F32):
    return jax.ShapeDtypeStruct(shape, dtype)


def up_from(group, steps):
    return (group + steps) % GRP


def down_from(group, steps):
    return (group + GRP - steps) % GRP


def aligned(value, unit):
    return pl.multiple_of(value * unit, unit)


def pack_body(where, trial, seabed, down, up, beside, last, first, bed, strips, edges, sems):
    edge = pl.ds(pl.multiple_of(jnp.where(where[1] == 0, CY - LANE, 0), LANE), LANE)
    moves = [
        (trial.at[:, :, CX - PAD :, :], last),
        (seabed, bed),
        (trial.at[:, :, :PAD, :], first),
        (trial.at[:, :, :, edge], edges.at[:MEM]),
        (strips.at[0], down),
        (strips.at[1], up),
        (edges, beside),
    ]
    copies = [pltpu.make_async_copy(*move, sems.at[i]) for i, move in enumerate(moves)]
    for copy in copies[:4]:
        copy.start()
    for side, (rows, end) in enumerate(((last, True), (first, False))):
        if end:
            copies[0].wait()
            copies[1].wait()
        else:
            copies[2].wait()
        base, sign = (CX - PAD, 0.5) if end else (0, -0.5)

        def take(first, count):
            return slice(PAD - first - count, PAD - first) if end else slice(first, first + count)

        for part in range(PARTS):
            lanes = slice(part * LANE, (part + 1) * LANE)
            deep = bed[base : base + PAD, lanes]
            for member in range(MEM):
                level, east, north = (rows[member, f, :, lanes] for f in range(3))

                def put(slot, count, value):
                    to = pl.ds(slot * MEM + member, count, stride=MEM)
                    strips[side, part, to, :] = value

                flux, plus = north * deep, sign * (east * deep)
                near, far = take(3, 2), take(4, 2)
                put(0, DU, east[take(0, DU), :])
                put(DU + end, DV - 1, north[take(0, DV - 1), :])
                put(DU + (0 if end else DV - 1), 1, flux[take(DV - 1, 1), :])
                put(DU + DV + 2 * end, DL - 2, level[take(0, DL - 2), :])
                put(DU + DV + (0 if end else DL - 2), 2, level[near, :] + plus[far, :])
            to = (STRIP - 1) * MEM
            strips[side, part, to : to + MEM, :] = jnp.zeros((MEM, LANE), F32)
            strips[side, part, to : to + DU, :] = deep[take(0, DU), :]
        copies[4 + side].start()
    for same in range(3):
        edges[MEM, same] = bed[:, edge]
    copies[3].wait()
    for copy in copies[6:]:
        copy.start()
    for copy in copies[4:]:
        copy.wait()


def pack(where, trial, seabed):
    strip = shaped(PARTS, STRIP * MEM, LANE)
    rows = pltpu.VMEM((MEM, 3, PAD, CY), F32)
    return pl.pallas_call(
        pack_body,
        out_shape=[strip, strip, shaped(MEM + 1, 3, CX, LANE)],
        in_specs=[SMEM, ANY, ANY],
        out_specs=[ANY] * 3,
        scratch_shapes=[
            rows,
            rows,
            pltpu.VMEM((CX, CY), F32),
            pltpu.VMEM((2,) + strip.shape, F32),
            pltpu.VMEM((MEM + 1, 3, CX, LANE), F32),
            pltpu.SemaphoreType.DMA((7,)),
        ],
        compiler_params=pltpu.CompilerParams(vmem_limit_bytes=60 * 1024 * 1024),
    )(where, trial, seabed)


def row_at(row):
    return pl.ds(aligned(row, MEM), MEM)


def get(ref, row):
    at = row_at(row)
    return jnp.concatenate([ref[part, at, :] for part in range(PARTS + 1)], axis=1)


def put(ref, row, value):
    at = row_at(row)
    for part in range(PARTS + 1):
        ref[part, at, :] = value[:, part * LANE : (part + 1) * LANE]


def across(value):
    return pltpu.roll(value, WIDE - 1, 1) - pltpu.roll(value, 1, 1)


def move_level(fields, row, inside):
    level, east, north, depth = fields
    along = get(depth, row + 1) * get(east, row + 1) - get(depth, row - 1) * get(east, row - 1)
    spread = 0.5 * along + 0.5 * across(get(depth, row) * get(north, row))
    put(level, row, (get(level, row) - spread) * inside)


def move_flow(fields, row):
    level, east, north, _ = fields
    slope = get(level, row + 1) - get(level, row - 1)
    put(east, row, (1.0 - FRICTION) * get(east, row) - 0.5 * slope)
    slope = across(get(level, row))
    put(north, row, (1.0 - FRICTION) * get(north, row) - 0.5 * slope)


def kept_half(core):
    lane = lax.broadcasted_iota(jnp.int32, (1, LANE), 1)
    return jnp.where((lane < LANE // 2) == (core == 0), 1.0, 0.0).astype(F32)


def inside_of(core):
    lane = lax.broadcasted_iota(jnp.int32, (1, WIDE), 1)
    inside = (lane < CY) | ((lane < CY + LANE // 2) == (core == 0))
    return jnp.where(inside, 1.0, 0.0).astype(F32)


def inner_body(where, trial, seabed, beside, *outs):
    blocks, fields = outs[:GRP], [outs[GRP].at[f] for f in range(4)]
    keep, inside = kept_half(where[1]), inside_of(where[1])
    for field in range(3):
        for member in range(MEM):
            at = pl.ds(member, CX, stride=MEM)
            for part in range(PARTS):
                fields[field][part, at, :] = trial[
                    member, field, :, part * LANE : (part + 1) * LANE
                ]
            fields[field][PARTS, at, :] = beside[member, field] * keep
    depth = fields[3]
    for row in range(CX):
        at = slice(row * MEM, (row + 1) * MEM)
        for part in range(PARTS):
            depth[part, at, :] = jnp.broadcast_to(
                seabed[row : row + 1, part * LANE : (part + 1) * LANE], (MEM, LANE)
            )
        depth[PARTS, at, :] = jnp.broadcast_to(
            beside[MEM, 0, row : row + 1, :] * keep, (MEM, LANE)
        )

    def level_row(row, carry):
        move_level(fields, row, inside)
        return carry

    def flow_row(row, carry):
        move_flow(fields, row)
        return carry

    for step in range(STEPS):
        lax.fori_loop(2 * step + 1, CX - 2 * step - 1, level_row, 0, unroll=2)
        lax.fori_loop(2 * step + 2, CX - 2 * step - 2, flow_row, 0, unroll=2)
    for other in range(GRP):
        for field in range(3):
            blocks[other][field * MIDDLE : (field + 1) * MIDDLE, :] = fields[field][
                up_from(where[0], other), HALF : CX * MEM - HALF, :
            ]


def inner_forecast(where, trial, seabed, beside):
    fields = shaped(4, PARTS + 1, CX * MEM, LANE)
    block = shaped(3 * MIDDLE, LANE)
    return call(
        inner_body,
        (block,) * GRP + (fields,),
        (where, trial, seabed, beside),
        flops=10_000_000,
        moved=32_000_000,
    )


def sense(levels, stencils):
    anchor = stencils[0:1, :].astype(jnp.int32)
    lane = lax.broadcasted_iota(jnp.int32, (1, LANE), 1)
    of_group = (lane % (GRP * OBS)) // OBS
    row = anchor // CY + of_group * (CX // GRP)
    pick = lax.broadcasted_iota(jnp.int32, (CY, LANE), 0) == anchor % CY
    pick = jnp.where(pick, 1.0, 0.0).astype(BF16)
    first = levels.astype(BF16)
    left = levels - first.astype(F32)
    second = left.astype(BF16)
    third = (left - second.astype(F32)).astype(BF16)
    dot = functools.partial(jnp.dot, preferred_element_type=F32)
    picked = dot(first, pick) + dot(second, pick) + dot(third, pick)
    total = jnp.zeros((MEM, LANE), F32)
    for at in range(CX):
        here = jnp.where(row == at, stencils[1:2, :], 0.0)
        here += jnp.where(row + 1 == at, stencils[2:3, :], 0.0)
        total += picked[at * MEM : (at + 1) * MEM, :] * here
    return total + pltpu.roll(total, LANE // 2, 1)


def outer_body(where, inner, above, below, corner, known, *rest):
    stencils, rest = rest[:GRP], rest[GRP:]
    blocks, state, whole, scratch = rest[:GRP], rest[GRP], rest[GRP + 1], rest[GRP + 2 :]
    group, core = where[0], where[1]
    keep, inside = kept_half(core), inside_of(core)
    given = [inner.at[f] for f in range(4)]
    half = HALF
    top, bottom = scratch[:4], scratch[4:]
    for field in range(4):
        for part in range(PARTS + 1):
            top[field][part, half:, :] = given[field][part, :half, :]
            bottom[field][part, :half, :] = given[field][part, CX * MEM - half :, :]
    for strip, side, fields in ((above, 0, top), (below, 1, bottom)):
        for part in range(PARTS + 1):

            def piece(low, count):
                if part < PARTS:
                    return strip[part, low : low + count, :]
                return corner[side, low : low + count, :] * keep

            at = 0
            for field, count in ((1, DU), (2, DV), (0, DL)):
                to = half if side else (PAD - count) * MEM
                fields[field][part, to : to + count * MEM, :] = piece(at * MEM, count * MEM)
                at += count
            for row in range(DU):
                to = half + row * MEM if side else (PAD - DU + row) * MEM
                fields[3][part, to : to + MEM, :] = jnp.broadcast_to(
                    piece((STRIP - 1) * MEM + row, 1), (MEM, LANE)
                )
            for beyond in (DU, DU + 1):
                to = half + beyond * MEM if side else half - (beyond + 1) * MEM
                fields[1][part, to : to + MEM, :] = jnp.zeros((MEM, LANE), F32)
                fields[3][part, to : to + MEM, :] = jnp.full((MEM, LANE), 1.0 * (beyond == DU), F32)
    has_above = inside * where[2].astype(F32)
    has_below = inside * where[3].astype(F32)
    for step in range(STEPS):
        shift = 2 * step
        for row in range(-5 + shift, 1 + shift):
            move_level(top, PAD + row, has_above if row < 0 else inside)
            move_level(bottom, PAD - 1 - row, has_below if row < 0 else inside)
        for row in range(-4 + shift, 2 + shift):
            move_flow(top, PAD + row)
            move_flow(bottom, PAD - 1 - row)

    levels = jnp.concatenate(
        [
            jnp.concatenate(
                [
                    top[0][part, half:, :],
                    given[0][part, half : CX * MEM - half, :],
                    bottom[0][part, :half, :],
                ],
                axis=0,
            )
            for part in range(PARTS)
        ],
        axis=1,
    )
    total = sense(levels, sum(s[...] for s in stencils))
    lane = lax.broadcasted_iota(jnp.int32, (1, LANE), 1)
    total = jnp.where(lane < GRP * OBS, total[: MEM // 2, :], total[MEM // 2 :, :])
    for to in range(GRP * SUB * 2):
        state[3 * to] = total
        state[3 * to + 1] = known[0]
        state[3 * to + 2] = known[1]

    for field in range(3):
        for part in range(PARTS):
            whole[field, part, :half, :] = top[field][part, half:, :]
            whole[field, part, half:, :] = bottom[field][part, :half, :]
        for other in range(GRP):
            blocks[other][field * MIDDLE : (field + 1) * MIDDLE, :] = whole[
                field, up_from(group, other)
            ]


def outer_forecast(where, inner, strips, known, stencils):
    block = shaped(3 * MIDDLE, LANE)
    return call(
        outer_body,
        (block,) * GRP
        + (shaped(3 * GRP * SUB * 2, MEM // 2, LANE), shaped(3, PARTS, 2 * HALF, LANE)),
        (where, inner, *strips, known, *stencils),
        [pltpu.VMEM((PARTS + 1, 2 * PAD * MEM, LANE), F32)] * 8,
    )


def turned_rows(block, field, member):
    return block[pl.ds(field * CX * MEM + member, CX, stride=MEM), :]


def unpack_body(where, *refs):
    blocks, out = refs[:-1], refs[-1]
    for other, block in zip(EARLY, blocks):
        at = pl.ds(aligned(down_from(where[0], other), LANE), LANE)
        for field in range(3):
            for member in range(MEM):
                out[member, field, :, at] = turned_rows(block, field, member)


def unpack_last_body(where, block, _, out, held, sem):
    for field in range(3):
        for member in range(MEM):
            held[member, field] = turned_rows(block, field, member)
    at = pl.ds(aligned(down_from(where[0], LATE), LANE), LANE)
    copy = pltpu.make_async_copy(held, out.at[:, :, :, at], sem)
    copy.start()
    copy.wait()


def unpack(where, blocks):
    out = shaped(MEM, 3, CX, CY)
    early = call(unpack_body, (out,), (where, *[blocks[s] for s in EARLY]))[0]
    return pl.pallas_call(
        unpack_last_body,
        out_shape=out,
        in_specs=[SMEM, VMEM, ANY],
        out_specs=ANY,
        scratch_shapes=[pltpu.VMEM((MEM, 3, CX, LANE), F32), pltpu.SemaphoreType.DMA],
        input_output_aliases={2: 0},
        compiler_params=pltpu.CompilerParams(vmem_limit_bytes=16 * 1024 * 1024),
    )(where, blocks[LATE], early)


def spread_out_body(where, inner, outer, out):
    for part in range(PARTS):
        lanes = slice(part * LANE, (part + 1) * LANE)
        for field in range(3):
            for member in range(MEM):
                out[member, field, PAD : CX - PAD, lanes] = inner[
                    field, part, pl.ds(HALF + member, CX - 2 * PAD, stride=MEM), :
                ]
                out[member, field, :PAD, lanes] = outer[
                    field, part, pl.ds(member, PAD, stride=MEM), :
                ]
                out[member, field, CX - PAD :, lanes] = outer[
                    field, part, pl.ds(HALF + member, PAD, stride=MEM), :
                ]


def spread_out(where, inner, outer):
    return call(spread_out_body, (shaped(MEM, 3, CX, CY),), (where, inner, outer))[0]


def products_body(where, states, out, seen_at, wanted_at):
    group = where[0]
    lane = lax.broadcasted_iota(jnp.int32, (1, LANE), 1)

    def unfolded(at):
        value = states[at]
        return jnp.concatenate([value, pltpu.roll(value, LANE // 2, 1)], axis=0)

    left, right = [], []
    for block in range(SUB * 2):
        noisy = [jnp.zeros((MEM, LANE), F32)] * GRP
        other = jnp.zeros((MEM // 2, LANE), F32)
        for source in range(GRP):
            at = 3 * (source * (SUB * 2) + block)
            held, here = unfolded(at + 1), lane // OBS == source
            for part in range(GRP):
                turned = pltpu.roll(held, (source - part) * OBS % LANE, 1)
                noisy[part] = jnp.where(here, turned, noisy[part])
            other = jnp.where(here, pltpu.roll(states[at + 2], source * OBS, 1), other)
        seen = [unfolded(3 * (source * (SUB * 2) + block)) for source in range(GRP)]
        for source in range(GRP):
            wanted_at[block, source] = noisy[source] - seen[source]
            seen_at[block, source] = seen[source]
        seen = [seen_at[block, down_from(group, s)] for s in range(GRP)]
        wanted = [wanted_at[block, up_from(group, s)] for s in range(GRP)]
        seen, wanted = jnp.concatenate(seen, axis=0), jnp.concatenate(wanted, axis=0)
        anomaly = seen - jnp.mean(seen, axis=0, keepdims=True)
        scaled = anomaly / jnp.where(lane < GRP * OBS, other[3:4, :], 1.0)
        left.append(jnp.concatenate([scaled * other[r : r + 1, :] for r in range(3)], axis=0))
        right.append(jnp.concatenate([anomaly, wanted], axis=0))
    out[...] = lax.dot_general(
        jnp.concatenate(left, axis=1),
        jnp.concatenate(right, axis=1),
        (((1,), (1,)), ((), ())),
        precision=HIGHEST,
        preferred_element_type=F32,
    )


def region_products(where, states):
    return call(
        products_body,
        (shaped(3 * E, 2 * E),),
        (where, states),
        [pltpu.VMEM((SUB * 2, GRP, MEM, LANE), F32)] * 2,
    )[0]


def solve_body(where, own, low, high, out):
    total = own[E : 2 * E, :] + low[...] + high[...]
    row = lax.broadcasted_iota(jnp.int32, (E, 2 * E), 0)
    lane = lax.broadcasted_iota(jnp.int32, (E, 2 * E), 1)
    system = total + jnp.where(row == lane, E - 1.0, 0.0)
    for k in range(E):
        pivot = system[k : k + 1, :] / system[k : k + 1, k : k + 1]
        system = jnp.where(row == k, pivot, system - system[:, k : k + 1] * pivot)
    out[...] = system[:, E:]


def solve(where, own, low, high):
    return call(solve_body, (shaped(E, E),), (where, own, low, high))[0]


def increments_body(where, *refs):
    weights, middle, edge, outs = refs[0], refs[1 : 1 + GRP], refs[1 + GRP : 1 + 2 * GRP], refs[1 + 2 * GRP :]
    turned = weights[...].T
    coarse = turned.astype(BF16)
    fine = (turned - coarse.astype(F32)).astype(BF16)
    left = jnp.concatenate([coarse, coarse, fine], axis=1)

    def some(blocks, low, to):
        pieces = []
        for row in range(PAD):
            at = slice(low + row * MEM, low + (row + 1) * MEM)
            pieces.append(jnp.concatenate([block[at, :] for block in blocks], axis=0))
        state = jnp.concatenate(pieces, axis=1)
        state = state - jnp.mean(state, axis=0, keepdims=True)
        high = state.astype(BF16)
        low_part = (state - high.astype(F32)).astype(BF16)
        right = jnp.concatenate([high, low_part, high], axis=0)
        result = jnp.dot(left, right, preferred_element_type=F32)
        for row in range(PAD):
            for other in range(GRP):
                outs[other][to + row * MEM : to + (row + 1) * MEM, :] = result[
                    other * MEM : (other + 1) * MEM, row * LANE : (row + 1) * LANE
                ]

    for field in range(3):
        at, to = field * MIDDLE, field * CX * MEM
        some(edge, at, to)
        some(middle, at, to + HALF)
        some(middle, at + HALF, to + 2 * HALF)
        some(edge, at + HALF, to + 3 * HALF)


def increments(where, weights, middle, edge):
    return call(
        increments_body,
        (shaped(3 * CX * MEM, LANE),) * GRP,
        (where, weights, *middle, *edge),
    )


def exchange(blocks):
    moved = {
        s: lax.ppermute(blocks[s], "grp", [(i, (i + s) % GRP) for i in range(GRP)]) for s in range(1, GRP)
    }
    return [blocks[0]] + [moved[s] for s in range(1, GRP)]


def on_device(
    trial, seabed, observed, variances, perturbations, stencil_cells, stencil_weights, region_mask
):
    group, region = lax.axis_index("grp"), lax.axis_index("reg")
    sub, core = lax.axis_index("sub"), lax.axis_index("cores")
    tile = region * SUB + sub
    where = jnp.stack(
        [group, core, (tile > 0).astype(jnp.int32), (tile < REG * SUB - 1).astype(jnp.int32)]
    ).astype(jnp.int32)
    forward = [(i, i + 1) for i in range(REG * SUB - 1)]
    backward = [(i + 1, i) for i in range(REG * SUB - 1)]

    down, up, beside = pack(where, trial, seabed)
    above = lax.ppermute(down, TILE, forward)
    below = lax.ppermute(up, TILE, backward)
    beside = lax.ppermute(beside, "cores", [(0, 1), (1, 0)])

    count = GRP * OBS
    anchor = stencil_cells[:, 0].astype(F32)
    pair = jnp.stack([anchor, anchor + 1.0])
    uses = stencil_weights.T
    stencil = jnp.stack([pair, uses[:2], uses[2:]])
    slot = (jnp.arange(GRP) == group).astype(F32)
    stencil = (stencil[:, :, None, :] * slot[None, None, :, None]).reshape(3, 2 * count)
    stencil = jnp.pad(stencil, ((0, MEM - 3), (0, 0)))
    noisy = observed[:, None] + jnp.sqrt(variances)[:, None] * perturbations
    noisy = noisy.T.reshape(GRP, 2, MEM // 2, OBS).transpose(2, 1, 0, 3).reshape(MEM // 2, LANE)
    three = lax.dynamic_slice_in_dim(
        jnp.pad(region_mask.astype(F32), ((0, 0), (1, 1))), region, 3, axis=1
    )
    three = jnp.concatenate([three.T, variances[None]], axis=0)
    known = jnp.stack([noisy, jnp.pad(three, ((0, 0), (0, LANE - OBS)))])

    stencil, beside = lax.optimization_barrier((stencil, beside))
    stencils = exchange([stencil] * GRP)
    *middle, inner = inner_forecast(where, trial, seabed, beside)
    above, below, _ = lax.optimization_barrier((above, below, stencils[1:]))

    def outer_rows(above, below, inner, known, stencils):
        edge = jnp.where(core == 0, PARTS - 1, 0)
        ends = [lax.dynamic_index_in_dim(s, edge, 0, keepdims=False) for s in (above, below)]
        corner = lax.ppermute(jnp.stack(ends), "cores", [(0, 1), (1, 0)])
        *outer, state, rest = outer_forecast(
            where, inner, (above, below, corner), known, stencils
        )
        return outer, rest, lax.all_to_all(state, SIDE, 0, 0, tiled=True)

    def nothing(*args):
        block = jnp.zeros((3 * MIDDLE, LANE), F32)
        rest = jnp.zeros((3, PARTS, 2 * HALF, LANE), F32)
        return [block] * GRP, rest, jnp.zeros((3 * GRP * SUB * 2, MEM // 2, LANE), F32)

    middle, *_ = lax.optimization_barrier((middle, stencils[1:]))
    middle = exchange(middle)
    outer, rest, states = lax.cond(
        group < GRP, outer_rows, nothing, above, below, inner, known, stencils
    )
    outer = exchange(outer)
    propagated_trials = spread_out(where, inner, rest)

    pairs = [
        (r * SUB + q, (r + 1) * SUB + (q ^ 2)) for r in range(REG - 1) for q in range(SUB)
    ]
    products = region_products(where, states)
    products, _ = lax.optimization_barrier((products, middle[1:]))
    from_above = lax.ppermute(products[2 * E :], TILE, pairs)
    from_below = lax.ppermute(products[:E], TILE, [(b, a) for a, b in pairs])
    weights = solve(where, products, from_above, from_below)
    analysis_updates = unpack(where, exchange(increments(where, weights, middle, outer)))
    return (propagated_trials, analysis_updates)


def solution(mesh):
    fine = Mesh(
        mesh.devices.reshape(GRP, REG, SUB, 2), ("grp", "reg", "sub", "cores")
    )
    every = ("grp", "reg", "sub", "cores")
    state = P("grp", None, TILE, "cores")
    in_specs = (
        state,
        P(TILE, "cores"),
        P(every),
        P(every),
        P(every, None),
        P(every, None),
        P(every, None),
        P(every, None),
    )
    return jax.shard_map(
        on_device, mesh=fine, in_specs=in_specs, out_specs=(state, state), check_vma=False
    )
```

```python
import functools

import jax
import jax.numpy as jnp
from jax import lax
from jax.experimental import pallas as pl
from jax.experimental.pallas import tpu as pltpu
from jax.sharding import Mesh, PartitionSpec as P

STEPS = 3
REG = 8
GRP = 4
SUB = 4
MEM = 8
E = 32
CX = 32
CY = 512
LANE = 128
PARTS = CY // LANE
WIDE = CY + LANE
PAD = 8
OBS = 16
HALF = PAD * MEM
MIDDLE = CX * MEM - 2 * HALF
DU, DV, DL = 4, 5, 5
STRIP = DU + DV + DL + 1
FRICTION = 0.02
HIGHEST = lax.Precision.HIGHEST
F32 = jnp.float32
BF16 = jnp.bfloat16
SIDE = ("grp", "sub", "cores")
TILE = ("reg", "sub")


VMEM = pl.BlockSpec(memory_space=pltpu.VMEM)
SMEM = pl.BlockSpec(memory_space=pltpu.SMEM)
ANY = pl.BlockSpec(memory_space=pl.ANY)


def call(body, outs, args, scratch=(), mib=16, flops=0, moved=0):
    return pl.pallas_call(
        body,
        out_shape=list(outs),
        in_specs=[SMEM] + [VMEM] * (len(args) - 1),
        out_specs=[VMEM] * len(outs),
        scratch_shapes=list(scratch),
        compiler_params=pltpu.CompilerParams(vmem_limit_bytes=mib * 1024 * 1024),
        cost_estimate=pl.CostEstimate(flops=flops, bytes_accessed=moved, transcendentals=0),
    )(*args)


def shaped(*shape, dtype=F32):
    return jax.ShapeDtypeStruct(shape, dtype)


def up_from(group, steps):
    return (group + steps) % GRP


def down_from(group, steps):
    return (group + GRP - steps) % GRP


def aligned(value, unit):
    return pl.multiple_of(value * unit, unit)


def pack_body(where, trial, seabed, down, up, beside, last, first, bed, strips, edges, sems):
    edge = pl.ds(pl.multiple_of(jnp.where(where[1] == 0, CY - LANE, 0), LANE), LANE)
    moves = [
        (trial.at[:, :, CX - PAD :, :], last),
        (seabed, bed),
        (trial.at[:, :, :PAD, :], first),
        (trial.at[:, :, :, edge], edges.at[:MEM]),
        (strips.at[0], down),
        (strips.at[1], up),
        (edges, beside),
    ]
    copies = [pltpu.make_async_copy(*move, sems.at[i]) for i, move in enumerate(moves)]
    for copy in copies[:4]:
        copy.start()
    for side, (rows, end) in enumerate(((last, True), (first, False))):
        if end:
            copies[0].wait()
            copies[1].wait()
        else:
            copies[2].wait()
        base, sign = (CX - PAD, 0.5) if end else (0, -0.5)

        def take(first, count):
            return slice(PAD - first - count, PAD - first) if end else slice(first, first + count)

        for part in range(PARTS):
            lanes = slice(part * LANE, (part + 1) * LANE)
            deep = bed[base : base + PAD, lanes]
            for member in range(MEM):
                level, east, north = (rows[member, f, :, lanes] for f in range(3))

                def put(slot, count, value):
                    to = pl.ds(slot * MEM + member, count, stride=MEM)
                    strips[side, part, to, :] = value

                flux, plus = north * deep, sign * (east * deep)
                near, far = take(3, 2), take(4, 2)
                put(0, DU, east[take(0, DU), :])
                put(DU + end, DV - 1, north[take(0, DV - 1), :])
                put(DU + (0 if end else DV - 1), 1, flux[take(DV - 1, 1), :])
                put(DU + DV + 2 * end, DL - 2, level[take(0, DL - 2), :])
                put(DU + DV + (0 if end else DL - 2), 2, level[near, :] + plus[far, :])
            to = (STRIP - 1) * MEM
            strips[side, part, to : to + MEM, :] = jnp.zeros((MEM, LANE), F32)
            strips[side, part, to : to + DU, :] = deep[take(0, DU), :]
        copies[4 + side].start()
    for same in range(3):
        edges[MEM, same] = bed[:, edge]
    copies[3].wait()
    for copy in copies[6:]:
        copy.start()
    for copy in copies[4:]:
        copy.wait()


def pack(where, trial, seabed):
    strip = shaped(PARTS, STRIP * MEM, LANE)
    rows = pltpu.VMEM((MEM, 3, PAD, CY), F32)
    return pl.pallas_call(
        pack_body,
        out_shape=[strip, strip, shaped(MEM + 1, 3, CX, LANE)],
        in_specs=[SMEM, ANY, ANY],
        out_specs=[ANY] * 3,
        scratch_shapes=[
            rows,
            rows,
            pltpu.VMEM((CX, CY), F32),
            pltpu.VMEM((2,) + strip.shape, F32),
            pltpu.VMEM((MEM + 1, 3, CX, LANE), F32),
            pltpu.SemaphoreType.DMA((7,)),
        ],
        compiler_params=pltpu.CompilerParams(vmem_limit_bytes=60 * 1024 * 1024),
    )(where, trial, seabed)


def row_at(row):
    return pl.ds(aligned(row, MEM), MEM)


def get(ref, row):
    at = row_at(row)
    return jnp.concatenate([ref[part, at, :] for part in range(PARTS + 1)], axis=1)


def put(ref, row, value):
    at = row_at(row)
    for part in range(PARTS + 1):
        ref[part, at, :] = value[:, part * LANE : (part + 1) * LANE]


def across(value):
    return pltpu.roll(value, WIDE - 1, 1) - pltpu.roll(value, 1, 1)


def move_level(fields, row, inside):
    level, east, north, depth = fields
    along = get(depth, row + 1) * get(east, row + 1) - get(depth, row - 1) * get(east, row - 1)
    spread = 0.5 * along + 0.5 * across(get(depth, row) * get(north, row))
    put(level, row, (get(level, row) - spread) * inside)


def move_flow(fields, row):
    level, east, north, _ = fields
    slope = get(level, row + 1) - get(level, row - 1)
    put(east, row, (1.0 - FRICTION) * get(east, row) - 0.5 * slope)
    slope = across(get(level, row))
    put(north, row, (1.0 - FRICTION) * get(north, row) - 0.5 * slope)


def kept_half(core):
    lane = lax.broadcasted_iota(jnp.int32, (1, LANE), 1)
    return jnp.where((lane < LANE // 2) == (core == 0), 1.0, 0.0).astype(F32)


def inside_of(core):
    lane = lax.broadcasted_iota(jnp.int32, (1, WIDE), 1)
    inside = (lane < CY) | ((lane < CY + LANE // 2) == (core == 0))
    return jnp.where(inside, 1.0, 0.0).astype(F32)


def inner_body(where, trial, seabed, beside, *outs):
    blocks, fields = outs[:GRP], [outs[GRP].at[f] for f in range(4)]
    keep, inside = kept_half(where[1]), inside_of(where[1])
    for field in range(3):
        for member in range(MEM):
            at = pl.ds(member, CX, stride=MEM)
            for part in range(PARTS):
                fields[field][part, at, :] = trial[
                    member, field, :, part * LANE : (part + 1) * LANE
                ]
            fields[field][PARTS, at, :] = beside[member, field] * keep
    depth = fields[3]
    for row in range(CX):
        at = slice(row * MEM, (row + 1) * MEM)
        for part in range(PARTS):
            depth[part, at, :] = jnp.broadcast_to(
                seabed[row : row + 1, part * LANE : (part + 1) * LANE], (MEM, LANE)
            )
        depth[PARTS, at, :] = jnp.broadcast_to(
            beside[MEM, 0, row : row + 1, :] * keep, (MEM, LANE)
        )

    def level_row(row, carry):
        move_level(fields, row, inside)
        return carry

    def flow_row(row, carry):
        move_flow(fields, row)
        return carry

    for step in range(STEPS):
        lax.fori_loop(2 * step + 1, CX - 2 * step - 1, level_row, 0, unroll=2)
        lax.fori_loop(2 * step + 2, CX - 2 * step - 2, flow_row, 0, unroll=2)
    for other in range(GRP):
        for field in range(3):
            blocks[other][field * MIDDLE : (field + 1) * MIDDLE, :] = fields[field][
                up_from(where[0], other), HALF : CX * MEM - HALF, :
            ]


def inner_forecast(where, trial, seabed, beside):
    fields = shaped(4, PARTS + 1, CX * MEM, LANE)
    block = shaped(3 * MIDDLE, LANE)
    return call(
        inner_body,
        (block,) * GRP + (fields,),
        (where, trial, seabed, beside),
        flops=10_000_000,
        moved=32_000_000,
    )


def sense(levels, stencils):
    anchor = stencils[0:1, :].astype(jnp.int32)
    lane = lax.broadcasted_iota(jnp.int32, (1, LANE), 1)
    of_group = (lane % (GRP * OBS)) // OBS
    row = anchor // CY + of_group * (CX // GRP)
    pick = lax.broadcasted_iota(jnp.int32, (CY, LANE), 0) == anchor % CY
    pick = jnp.where(pick, 1.0, 0.0).astype(BF16)
    first = levels.astype(BF16)
    left = levels - first.astype(F32)
    second = left.astype(BF16)
    third = (left - second.astype(F32)).astype(BF16)
    dot = functools.partial(jnp.dot, preferred_element_type=F32)
    picked = dot(first, pick) + dot(second, pick) + dot(third, pick)
    total = jnp.zeros((MEM, LANE), F32)
    for at in range(CX):
        here = jnp.where(row == at, stencils[1:2, :], 0.0)
        here += jnp.where(row + 1 == at, stencils[2:3, :], 0.0)
        total += picked[at * MEM : (at + 1) * MEM, :] * here
    return total + pltpu.roll(total, LANE // 2, 1)


def outer_body(where, inner, above, below, corner, known, *rest):
    stencils, rest = rest[:GRP], rest[GRP:]
    blocks, state, whole, scratch = rest[:GRP], rest[GRP], rest[GRP + 1], rest[GRP + 2 :]
    group, core = where[0], where[1]
    keep, inside = kept_half(core), inside_of(core)
    given = [inner.at[f] for f in range(4)]
    half = HALF
    top, bottom = scratch[:4], scratch[4:]
    for field in range(4):
        for part in range(PARTS + 1):
            top[field][part, half:, :] = given[field][part, :half, :]
            bottom[field][part, :half, :] = given[field][part, CX * MEM - half :, :]
    for strip, side, fields in ((above, 0, top), (below, 1, bottom)):
        for part in range(PARTS + 1):

            def piece(low, count):
                if part < PARTS:
                    return strip[part, low : low + count, :]
                return corner[side, low : low + count, :] * keep

            at = 0
            for field, count in ((1, DU), (2, DV), (0, DL)):
                to = half if side else (PAD - count) * MEM
                fields[field][part, to : to + count * MEM, :] = piece(at * MEM, count * MEM)
                at += count
            for row in range(DU):
                to = half + row * MEM if side else (PAD - DU + row) * MEM
                fields[3][part, to : to + MEM, :] = jnp.broadcast_to(
                    piece((STRIP - 1) * MEM + row, 1), (MEM, LANE)
                )
            for beyond in (DU, DU + 1):
                to = half + beyond * MEM if side else half - (beyond + 1) * MEM
                fields[1][part, to : to + MEM, :] = jnp.zeros((MEM, LANE), F32)
                fields[3][part, to : to + MEM, :] = jnp.full((MEM, LANE), 1.0 * (beyond == DU), F32)
    has_above = inside * where[2].astype(F32)
    has_below = inside * where[3].astype(F32)
    for step in range(STEPS):
        shift = 2 * step
        for row in range(-5 + shift, 1 + shift):
            move_level(top, PAD + row, has_above if row < 0 else inside)
            move_level(bottom, PAD - 1 - row, has_below if row < 0 else inside)
        for row in range(-4 + shift, 2 + shift):
            move_flow(top, PAD + row)
            move_flow(bottom, PAD - 1 - row)

    levels = jnp.concatenate(
        [
            jnp.concatenate(
                [
                    top[0][part, half:, :],
                    given[0][part, half : CX * MEM - half, :],
                    bottom[0][part, :half, :],
                ],
                axis=0,
            )
            for part in range(PARTS)
        ],
        axis=1,
    )
    total = sense(levels, sum(s[...] for s in stencils))
    lane = lax.broadcasted_iota(jnp.int32, (1, LANE), 1)
    total = jnp.where(lane < GRP * OBS, total[: MEM // 2, :], total[MEM // 2 :, :])
    for to in range(GRP * SUB * 2):
        state[3 * to] = total
        state[3 * to + 1] = known[0]
        state[3 * to + 2] = known[1]

    for field in range(3):
        for part in range(PARTS):
            whole[field, part, :half, :] = top[field][part, half:, :]
            whole[field, part, half:, :] = bottom[field][part, :half, :]
        for other in range(GRP):
            blocks[other][field * MIDDLE : (field + 1) * MIDDLE, :] = whole[
                field, up_from(group, other)
            ]


def outer_forecast(where, inner, strips, known, stencils):
    block = shaped(3 * MIDDLE, LANE)
    return call(
        outer_body,
        (block,) * GRP
        + (shaped(3 * GRP * SUB * 2, MEM // 2, LANE), shaped(3, PARTS, 2 * HALF, LANE)),
        (where, inner, *strips, known, *stencils),
        [pltpu.VMEM((PARTS + 1, 2 * PAD * MEM, LANE), F32)] * 8,
    )


def unpack_middle_body(where, *refs):
    blocks, out = refs[:GRP], refs[GRP]
    for other, block in enumerate(blocks):
        at = pl.ds(aligned(down_from(where[0], other), LANE), LANE)
        for field in range(3):
            for member in range(MEM):
                out[member, field, PAD : CX - PAD, at] = block[
                    pl.ds(field * MIDDLE + member, CX - 2 * PAD, stride=MEM), :
                ]


def unpack_outer_body(where, *refs):
    blocks, (_, out, held, sems) = refs[:GRP], refs[GRP:]
    copies = [
        pltpu.make_async_copy(held.at[side], out.at[:, :, rows, :], sems.at[side])
        for side, rows in enumerate((pl.ds(0, PAD), pl.ds(CX - PAD, PAD)))
    ]
    for side in range(2):
        for other, block in enumerate(blocks):
            at = pl.ds(aligned(down_from(where[0], other), LANE), LANE)
            for field in range(3):
                for member in range(MEM):
                    low = field * MIDDLE + side * HALF + member
                    held[side, member, field, :, at] = block[pl.ds(low, PAD, stride=MEM), :]
        copies[side].start()
    for copy in copies:
        copy.wait()


def unpack(where, middle, outer):
    out = shaped(MEM, 3, CX, CY)
    early = call(unpack_middle_body, (out,), (where, *middle), flops=10_000_000, moved=32_000_000)
    return pl.pallas_call(
        unpack_outer_body,
        out_shape=out,
        in_specs=[SMEM] + [VMEM] * GRP + [ANY],
        out_specs=ANY,
        scratch_shapes=[
            pltpu.VMEM((2, MEM, 3, PAD, CY), F32),
            pltpu.SemaphoreType.DMA((2,)),
        ],
        input_output_aliases={1 + GRP: 0},
        compiler_params=pltpu.CompilerParams(vmem_limit_bytes=16 * 1024 * 1024),
    )(where, *outer, early[0])


def spread_out_body(where, inner, outer, out):
    for part in range(PARTS):
        lanes = slice(part * LANE, (part + 1) * LANE)
        for field in range(3):
            for member in range(MEM):
                out[member, field, PAD : CX - PAD, lanes] = inner[
                    field, part, pl.ds(HALF + member, CX - 2 * PAD, stride=MEM), :
                ]
                out[member, field, :PAD, lanes] = outer[
                    field, part, pl.ds(member, PAD, stride=MEM), :
                ]
                out[member, field, CX - PAD :, lanes] = outer[
                    field, part, pl.ds(HALF + member, PAD, stride=MEM), :
                ]


def spread_out(where, inner, outer):
    return call(spread_out_body, (shaped(MEM, 3, CX, CY),), (where, inner, outer))[0]


def products_body(where, states, out, seen_at, wanted_at):
    group = where[0]
    lane = lax.broadcasted_iota(jnp.int32, (1, LANE), 1)

    def unfolded(at):
        value = states[at]
        return jnp.concatenate([value, pltpu.roll(value, LANE // 2, 1)], axis=0)

    left, right = [], []
    for block in range(SUB * 2):
        noisy = [jnp.zeros((MEM, LANE), F32)] * GRP
        other = jnp.zeros((MEM // 2, LANE), F32)
        for source in range(GRP):
            at = 3 * (source * (SUB * 2) + block)
            held, here = unfolded(at + 1), lane // OBS == source
            for part in range(GRP):
                turned = pltpu.roll(held, (source - part) * OBS % LANE, 1)
                noisy[part] = jnp.where(here, turned, noisy[part])
            other = jnp.where(here, pltpu.roll(states[at + 2], source * OBS, 1), other)
        seen = [unfolded(3 * (source * (SUB * 2) + block)) for source in range(GRP)]
        for source in range(GRP):
            wanted_at[block, source] = noisy[source] - seen[source]
            seen_at[block, source] = seen[source]
        seen = [seen_at[block, down_from(group, s)] for s in range(GRP)]
        wanted = [wanted_at[block, up_from(group, s)] for s in range(GRP)]
        seen, wanted = jnp.concatenate(seen, axis=0), jnp.concatenate(wanted, axis=0)
        anomaly = seen - jnp.mean(seen, axis=0, keepdims=True)
        scaled = anomaly / jnp.where(lane < GRP * OBS, other[3:4, :], 1.0)
        left.append(jnp.concatenate([scaled * other[r : r + 1, :] for r in range(3)], axis=0))
        right.append(jnp.concatenate([anomaly, wanted], axis=0))
    out[...] = lax.dot_general(
        jnp.concatenate(left, axis=1),
        jnp.concatenate(right, axis=1),
        (((1,), (1,)), ((), ())),
        precision=HIGHEST,
        preferred_element_type=F32,
    )


def region_products(where, states):
    return call(
        products_body,
        (shaped(3 * E, 2 * E),),
        (where, states),
        [pltpu.VMEM((SUB * 2, GRP, MEM, LANE), F32)] * 2,
    )[0]


def solve_body(where, own, low, high, out):
    total = own[E : 2 * E, :] + low[...] + high[...]
    row = lax.broadcasted_iota(jnp.int32, (E, 2 * E), 0)
    lane = lax.broadcasted_iota(jnp.int32, (E, 2 * E), 1)
    system = total + jnp.where(row == lane, E - 1.0, 0.0)
    for k in range(E):
        pivot = system[k : k + 1, :] / system[k : k + 1, k : k + 1]
        system = jnp.where(row == k, pivot, system - system[:, k : k + 1] * pivot)
    out[...] = system[:, E:]


def solve(where, own, low, high):
    return call(solve_body, (shaped(E, E),), (where, own, low, high))[0]


def increments_body(where, weights, *refs):
    blocks, outs = refs[:GRP], refs[GRP:]
    turned = weights[...].T
    coarse = turned.astype(BF16)
    fine = (turned - coarse.astype(F32)).astype(BF16)
    left = jnp.concatenate([coarse, coarse, fine], axis=1)
    for low in range(0, 3 * MIDDLE, HALF):
        pieces = []
        for row in range(PAD):
            at = slice(low + row * MEM, low + (row + 1) * MEM)
            pieces.append(jnp.concatenate([block[at, :] for block in blocks], axis=0))
        state = jnp.concatenate(pieces, axis=1)
        state = state - jnp.mean(state, axis=0, keepdims=True)
        high = state.astype(BF16)
        low_part = (state - high.astype(F32)).astype(BF16)
        right = jnp.concatenate([high, low_part, high], axis=0)
        result = jnp.dot(left, right, preferred_element_type=F32)
        for row in range(PAD):
            for other in range(GRP):
                outs[other][low + row * MEM : low + (row + 1) * MEM, :] = result[
                    other * MEM : (other + 1) * MEM, row * LANE : (row + 1) * LANE
                ]


def increments(where, weights, blocks):
    return call(increments_body, (shaped(3 * MIDDLE, LANE),) * GRP, (where, weights, *blocks))


def exchange(blocks):
    moved = {
        s: lax.ppermute(blocks[s], "grp", [(i, (i + s) % GRP) for i in range(GRP)]) for s in range(1, GRP)
    }
    return [blocks[0]] + [moved[s] for s in range(1, GRP)]


def on_device(
    trial, seabed, observed, variances, perturbations, stencil_cells, stencil_weights, region_mask
):
    group, region = lax.axis_index("grp"), lax.axis_index("reg")
    sub, core = lax.axis_index("sub"), lax.axis_index("cores")
    tile = region * SUB + sub
    where = jnp.stack(
        [group, core, (tile > 0).astype(jnp.int32), (tile < REG * SUB - 1).astype(jnp.int32)]
    ).astype(jnp.int32)
    forward = [(i, i + 1) for i in range(REG * SUB - 1)]
    backward = [(i + 1, i) for i in range(REG * SUB - 1)]

    down, up, beside = pack(where, trial, seabed)
    above = lax.ppermute(down, TILE, forward)
    below = lax.ppermute(up, TILE, backward)
    beside = lax.ppermute(beside, "cores", [(0, 1), (1, 0)])

    count = GRP * OBS
    anchor = stencil_cells[:, 0].astype(F32)
    pair = jnp.stack([anchor, anchor + 1.0])
    uses = stencil_weights.T
    stencil = jnp.stack([pair, uses[:2], uses[2:]])
    slot = (jnp.arange(GRP) == group).astype(F32)
    stencil = (stencil[:, :, None, :] * slot[None, None, :, None]).reshape(3, 2 * count)
    stencil = jnp.pad(stencil, ((0, MEM - 3), (0, 0)))
    noisy = observed[:, None] + jnp.sqrt(variances)[:, None] * perturbations
    noisy = noisy.T.reshape(GRP, 2, MEM // 2, OBS).transpose(2, 1, 0, 3).reshape(MEM // 2, LANE)
    three = lax.dynamic_slice_in_dim(
        jnp.pad(region_mask.astype(F32), ((0, 0), (1, 1))), region, 3, axis=1
    )
    three = jnp.concatenate([three.T, variances[None]], axis=0)
    known = jnp.stack([noisy, jnp.pad(three, ((0, 0), (0, LANE - OBS)))])

    stencil, beside = lax.optimization_barrier((stencil, beside))
    stencils = exchange([stencil] * GRP)
    *middle, inner = inner_forecast(where, trial, seabed, beside)
    above, below, _ = lax.optimization_barrier((above, below, stencils[1:]))

    def outer_rows(above, below, inner, known, stencils):
        edge = jnp.where(core == 0, PARTS - 1, 0)
        ends = [lax.dynamic_index_in_dim(s, edge, 0, keepdims=False) for s in (above, below)]
        corner = lax.ppermute(jnp.stack(ends), "cores", [(0, 1), (1, 0)])
        *outer, state, rest = outer_forecast(
            where, inner, (above, below, corner), known, stencils
        )
        return outer, rest, lax.all_to_all(state, SIDE, 0, 0, tiled=True)

    def nothing(*args):
        block = jnp.zeros((3 * MIDDLE, LANE), F32)
        rest = jnp.zeros((3, PARTS, 2 * HALF, LANE), F32)
        return [block] * GRP, rest, jnp.zeros((3 * GRP * SUB * 2, MEM // 2, LANE), F32)

    middle, *_ = lax.optimization_barrier((middle, stencils[1:]))
    middle = exchange(middle)
    outer, rest, states = lax.cond(
        group < GRP, outer_rows, nothing, above, below, inner, known, stencils
    )
    pairs = [
        (r * SUB + q, (r + 1) * SUB + (q ^ 2)) for r in range(REG - 1) for q in range(SUB)
    ]

    def chain(states):
        products = region_products(where, states)
        from_above = lax.ppermute(products[2 * E :], TILE, pairs)
        from_below = lax.ppermute(products[:E], TILE, [(b, a) for a, b in pairs])
        return solve(where, products, from_above, from_below)

    states, outer, _ = lax.optimization_barrier((states, outer, middle[1:]))
    outer = exchange(outer)
    propagated_trials = spread_out(where, inner, rest)
    weights = lax.cond(group < GRP, chain, lambda states: jnp.zeros((E, E), F32), states)
    analysis_updates = unpack(
        where,
        exchange(increments(where, weights, middle)),
        exchange(increments(where, weights, outer)),
    )
    return (propagated_trials, analysis_updates)


def solution(mesh):
    fine = Mesh(
        mesh.devices.reshape(GRP, REG, SUB, 2), ("grp", "reg", "sub", "cores")
    )
    every = ("grp", "reg", "sub", "cores")
    state = P("grp", None, TILE, "cores")
    in_specs = (
        state,
        P(TILE, "cores"),
        P(every),
        P(every),
        P(every, None),
        P(every, None),
        P(every, None),
        P(every, None),
    )
    return jax.shard_map(
        on_device, mesh=fine, in_specs=in_specs, out_specs=(state, state), check_vma=False
    )
```

```python
import functools

import jax
import jax.numpy as jnp
from jax import lax
from jax.experimental import pallas as pl
from jax.experimental.pallas import tpu as pltpu
from jax.sharding import Mesh, PartitionSpec as P

STEPS = 3
REG = 8
GRP = 4
SUB = 4
MEM = 8
E = 32
CX = 32
CY = 512
LANE = 128
PARTS = CY // LANE
WIDE = CY + LANE
PAD = 8
OBS = 16
HALF = PAD * MEM
MIDDLE = CX * MEM - 2 * HALF
DU, DV, DL = 4, 5, 5
STRIP = DU + DV + DL + 1
FRICTION = 0.02
HIGHEST = lax.Precision.HIGHEST
F32 = jnp.float32
BF16 = jnp.bfloat16
SIDE = ("grp", "sub", "cores")
TILE = ("reg", "sub")


VMEM = pl.BlockSpec(memory_space=pltpu.VMEM)
SMEM = pl.BlockSpec(memory_space=pltpu.SMEM)
ANY = pl.BlockSpec(memory_space=pl.ANY)


def call(body, outs, args, scratch=(), mib=16, flops=0, moved=0):
    return pl.pallas_call(
        body,
        out_shape=list(outs),
        in_specs=[SMEM] + [VMEM] * (len(args) - 1),
        out_specs=[VMEM] * len(outs),
        scratch_shapes=list(scratch),
        compiler_params=pltpu.CompilerParams(vmem_limit_bytes=mib * 1024 * 1024),
        cost_estimate=pl.CostEstimate(flops=flops, bytes_accessed=moved, transcendentals=0),
    )(*args)


def shaped(*shape, dtype=F32):
    return jax.ShapeDtypeStruct(shape, dtype)


def up_from(group, steps):
    return (group + steps) % GRP


def down_from(group, steps):
    return (group + GRP - steps) % GRP


def aligned(value, unit):
    return pl.multiple_of(value * unit, unit)


def pack_body(where, trial, seabed, down, up, beside, last, first, bed, strips, edges, sems):
    edge = pl.ds(pl.multiple_of(jnp.where(where[1] == 0, CY - LANE, 0), LANE), LANE)
    moves = [
        (trial.at[:, :, CX - PAD :, :], last),
        (seabed, bed),
        (trial.at[:, :, :PAD, :], first),
        (trial.at[:, :, :, edge], edges.at[:MEM]),
        (strips.at[0], down),
        (strips.at[1], up),
        (edges, beside),
    ]
    copies = [pltpu.make_async_copy(*move, sems.at[i]) for i, move in enumerate(moves)]
    for copy in copies[:4]:
        copy.start()
    for side, (rows, end) in enumerate(((last, True), (first, False))):
        if end:
            copies[0].wait()
            copies[1].wait()
        else:
            copies[2].wait()
        base, sign = (CX - PAD, 0.5) if end else (0, -0.5)

        def take(first, count):
            return slice(PAD - first - count, PAD - first) if end else slice(first, first + count)

        for part in range(PARTS):
            lanes = slice(part * LANE, (part + 1) * LANE)
            deep = bed[base : base + PAD, lanes]
            for member in range(MEM):
                level, east, north = (rows[member, f, :, lanes] for f in range(3))

                def put(slot, count, value):
                    to = pl.ds(slot * MEM + member, count, stride=MEM)
                    strips[side, part, to, :] = value

                flux, plus = north * deep, sign * (east * deep)
                near, far = take(3, 2), take(4, 2)
                put(0, DU, east[take(0, DU), :])
                put(DU + end, DV - 1, north[take(0, DV - 1), :])
                put(DU + (0 if end else DV - 1), 1, flux[take(DV - 1, 1), :])
                put(DU + DV + 2 * end, DL - 2, level[take(0, DL - 2), :])
                put(DU + DV + (0 if end else DL - 2), 2, level[near, :] + plus[far, :])
            to = (STRIP - 1) * MEM
            strips[side, part, to : to + MEM, :] = jnp.zeros((MEM, LANE), F32)
            strips[side, part, to : to + DU, :] = deep[take(0, DU), :]
        copies[4 + side].start()
    for same in range(3):
        edges[MEM, same] = bed[:, edge]
    copies[3].wait()
    for copy in copies[6:]:
        copy.start()
    for copy in copies[4:]:
        copy.wait()


def pack(where, trial, seabed):
    strip = shaped(PARTS, STRIP * MEM, LANE)
    rows = pltpu.VMEM((MEM, 3, PAD, CY), F32)
    return pl.pallas_call(
        pack_body,
        out_shape=[strip, strip, shaped(MEM + 1, 3, CX, LANE)],
        in_specs=[SMEM, ANY, ANY],
        out_specs=[ANY] * 3,
        scratch_shapes=[
            rows,
            rows,
            pltpu.VMEM((CX, CY), F32),
            pltpu.VMEM((2,) + strip.shape, F32),
            pltpu.VMEM((MEM + 1, 3, CX, LANE), F32),
            pltpu.SemaphoreType.DMA((7,)),
        ],
        compiler_params=pltpu.CompilerParams(vmem_limit_bytes=60 * 1024 * 1024),
    )(where, trial, seabed)


def row_at(row):
    return pl.ds(aligned(row, MEM), MEM)


def get(ref, row):
    at = row_at(row)
    return jnp.concatenate([ref[part, at, :] for part in range(PARTS + 1)], axis=1)


def put(ref, row, value):
    at = row_at(row)
    for part in range(PARTS + 1):
        ref[part, at, :] = value[:, part * LANE : (part + 1) * LANE]


def across(value):
    return pltpu.roll(value, WIDE - 1, 1) - pltpu.roll(value, 1, 1)


def move_level(fields, row, inside):
    level, east, north, depth = fields
    along = get(depth, row + 1) * get(east, row + 1) - get(depth, row - 1) * get(east, row - 1)
    spread = 0.5 * along + 0.5 * across(get(depth, row) * get(north, row))
    put(level, row, (get(level, row) - spread) * inside)


def move_flow(fields, row):
    level, east, north, _ = fields
    slope = get(level, row + 1) - get(level, row - 1)
    put(east, row, (1.0 - FRICTION) * get(east, row) - 0.5 * slope)
    slope = across(get(level, row))
    put(north, row, (1.0 - FRICTION) * get(north, row) - 0.5 * slope)


def kept_half(core):
    lane = lax.broadcasted_iota(jnp.int32, (1, LANE), 1)
    return jnp.where((lane < LANE // 2) == (core == 0), 1.0, 0.0).astype(F32)


def inside_of(core):
    lane = lax.broadcasted_iota(jnp.int32, (1, WIDE), 1)
    inside = (lane < CY) | ((lane < CY + LANE // 2) == (core == 0))
    return jnp.where(inside, 1.0, 0.0).astype(F32)


def inner_body(where, trial, seabed, beside, *outs):
    blocks, fields = outs[:GRP], [outs[GRP].at[f] for f in range(4)]
    keep, inside = kept_half(where[1]), inside_of(where[1])
    for field in range(3):
        for member in range(MEM):
            at = pl.ds(member, CX, stride=MEM)
            for part in range(PARTS):
                fields[field][part, at, :] = trial[
                    member, field, :, part * LANE : (part + 1) * LANE
                ]
            fields[field][PARTS, at, :] = beside[member, field] * keep
    depth = fields[3]
    for row in range(CX):
        at = slice(row * MEM, (row + 1) * MEM)
        for part in range(PARTS):
            depth[part, at, :] = jnp.broadcast_to(
                seabed[row : row + 1, part * LANE : (part + 1) * LANE], (MEM, LANE)
            )
        depth[PARTS, at, :] = jnp.broadcast_to(
            beside[MEM, 0, row : row + 1, :] * keep, (MEM, LANE)
        )

    def level_row(row, carry):
        move_level(fields, row, inside)
        return carry

    def flow_row(row, carry):
        move_flow(fields, row)
        return carry

    for step in range(STEPS):
        lax.fori_loop(2 * step + 1, CX - 2 * step - 1, level_row, 0, unroll=2)
        lax.fori_loop(2 * step + 2, CX - 2 * step - 2, flow_row, 0, unroll=2)
    for other in range(GRP):
        for field in range(3):
            blocks[other][field * MIDDLE : (field + 1) * MIDDLE, :] = fields[field][
                up_from(where[0], other), HALF : CX * MEM - HALF, :
            ]


def inner_forecast(where, trial, seabed, beside):
    fields = shaped(4, PARTS + 1, CX * MEM, LANE)
    block = shaped(3 * MIDDLE, LANE)
    return call(
        inner_body,
        (block,) * GRP + (fields,),
        (where, trial, seabed, beside),
        flops=10_000_000,
        moved=32_000_000,
    )


def sense(levels, stencils):
    anchor = stencils[0:1, :].astype(jnp.int32)
    lane = lax.broadcasted_iota(jnp.int32, (1, LANE), 1)
    of_group = (lane % (GRP * OBS)) // OBS
    row = anchor // CY + of_group * (CX // GRP)
    pick = lax.broadcasted_iota(jnp.int32, (CY, LANE), 0) == anchor % CY
    pick = jnp.where(pick, 1.0, 0.0).astype(BF16)
    first = levels.astype(BF16)
    left = levels - first.astype(F32)
    second = left.astype(BF16)
    third = (left - second.astype(F32)).astype(BF16)
    dot = functools.partial(jnp.dot, preferred_element_type=F32)
    picked = dot(first, pick) + dot(second, pick) + dot(third, pick)
    total = jnp.zeros((MEM, LANE), F32)
    for at in range(CX):
        here = jnp.where(row == at, stencils[1:2, :], 0.0)
        here += jnp.where(row + 1 == at, stencils[2:3, :], 0.0)
        total += picked[at * MEM : (at + 1) * MEM, :] * here
    return total + pltpu.roll(total, LANE // 2, 1)


def outer_body(where, inner, above, below, corner, known, *rest):
    stencils, rest = rest[:GRP], rest[GRP:]
    blocks, state, whole, scratch = rest[:GRP], rest[GRP], rest[GRP + 1], rest[GRP + 2 :]
    group, core = where[0], where[1]
    keep, inside = kept_half(core), inside_of(core)
    given = [inner.at[f] for f in range(4)]
    half = HALF
    top, bottom = scratch[:4], scratch[4:]
    for field in range(4):
        for part in range(PARTS + 1):
            top[field][part, half:, :] = given[field][part, :half, :]
            bottom[field][part, :half, :] = given[field][part, CX * MEM - half :, :]
    for strip, side, fields in ((above, 0, top), (below, 1, bottom)):
        for part in range(PARTS + 1):

            def piece(low, count):
                if part < PARTS:
                    return strip[part, low : low + count, :]
                return corner[side, low : low + count, :] * keep

            at = 0
            for field, count in ((1, DU), (2, DV), (0, DL)):
                to = half if side else (PAD - count) * MEM
                fields[field][part, to : to + count * MEM, :] = piece(at * MEM, count * MEM)
                at += count
            for row in range(DU):
                to = half + row * MEM if side else (PAD - DU + row) * MEM
                fields[3][part, to : to + MEM, :] = jnp.broadcast_to(
                    piece((STRIP - 1) * MEM + row, 1), (MEM, LANE)
                )
            for beyond in (DU, DU + 1):
                to = half + beyond * MEM if side else half - (beyond + 1) * MEM
                fields[1][part, to : to + MEM, :] = jnp.zeros((MEM, LANE), F32)
                fields[3][part, to : to + MEM, :] = jnp.full((MEM, LANE), 1.0 * (beyond == DU), F32)
    has_above = inside * where[2].astype(F32)
    has_below = inside * where[3].astype(F32)
    for step in range(STEPS):
        shift = 2 * step
        for row in range(-5 + shift, 1 + shift):
            move_level(top, PAD + row, has_above if row < 0 else inside)
            move_level(bottom, PAD - 1 - row, has_below if row < 0 else inside)
        for row in range(-4 + shift, 2 + shift):
            move_flow(top, PAD + row)
            move_flow(bottom, PAD - 1 - row)

    levels = jnp.concatenate(
        [
            jnp.concatenate(
                [
                    top[0][part, half:, :],
                    given[0][part, half : CX * MEM - half, :],
                    bottom[0][part, :half, :],
                ],
                axis=0,
            )
            for part in range(PARTS)
        ],
        axis=1,
    )
    total = sense(levels, sum(s[...] for s in stencils))
    lane = lax.broadcasted_iota(jnp.int32, (1, LANE), 1)
    total = jnp.where(lane < GRP * OBS, total[: MEM // 2, :], total[MEM // 2 :, :])
    for to in range(GRP * SUB * 2):
        state[3 * to] = total
        state[3 * to + 1] = known[0]
        state[3 * to + 2] = known[1]

    for field in range(3):
        for part in range(PARTS):
            whole[field, part, :half, :] = top[field][part, half:, :]
            whole[field, part, half:, :] = bottom[field][part, :half, :]
        for other in range(GRP):
            blocks[other][field * MIDDLE : (field + 1) * MIDDLE, :] = whole[
                field, up_from(group, other)
            ]


def outer_forecast(where, inner, strips, known, stencils):
    block = shaped(3 * MIDDLE, LANE)
    return call(
        outer_body,
        (block,) * GRP
        + (shaped(3 * GRP * SUB * 2, MEM // 2, LANE), shaped(3, PARTS, 2 * HALF, LANE)),
        (where, inner, *strips, known, *stencils),
        [pltpu.VMEM((PARTS + 1, 2 * PAD * MEM, LANE), F32)] * 8,
    )


def unpack_middle_body(where, *refs):
    blocks, out = refs[:GRP], refs[GRP]
    for other, block in enumerate(blocks):
        at = pl.ds(aligned(down_from(where[0], other), LANE), LANE)
        for field in range(3):
            for member in range(MEM):
                out[member, field, PAD : CX - PAD, at] = block[
                    pl.ds(field * MIDDLE + member, CX - 2 * PAD, stride=MEM), :
                ]


def unpack_outer_body(where, *refs):
    blocks, (_, out, held, sems) = refs[:GRP], refs[GRP:]
    copies = [
        pltpu.make_async_copy(held.at[side], out.at[:, :, rows, :], sems.at[side])
        for side, rows in enumerate((pl.ds(0, PAD), pl.ds(CX - PAD, PAD)))
    ]
    for side in range(2):
        for other, block in enumerate(blocks):
            at = pl.ds(aligned(down_from(where[0], other), LANE), LANE)
            for field in range(3):
                for member in range(MEM):
                    low = field * MIDDLE + side * HALF + member
                    held[side, member, field, :, at] = block[pl.ds(low, PAD, stride=MEM), :]
        copies[side].start()
    for copy in copies:
        copy.wait()


def unpack(where, middle, outer):
    out = shaped(MEM, 3, CX, CY)
    early = call(unpack_middle_body, (out,), (where, *middle), flops=10_000_000, moved=32_000_000)
    return pl.pallas_call(
        unpack_outer_body,
        out_shape=out,
        in_specs=[SMEM] + [VMEM] * GRP + [ANY],
        out_specs=ANY,
        scratch_shapes=[
            pltpu.VMEM((2, MEM, 3, PAD, CY), F32),
            pltpu.SemaphoreType.DMA((2,)),
        ],
        input_output_aliases={1 + GRP: 0},
        compiler_params=pltpu.CompilerParams(vmem_limit_bytes=16 * 1024 * 1024),
    )(where, *outer, early[0])


def spread_out_body(where, inner, outer, out):
    for part in range(PARTS):
        lanes = slice(part * LANE, (part + 1) * LANE)
        for field in range(3):
            for member in range(MEM):
                out[member, field, PAD : CX - PAD, lanes] = inner[
                    field, part, pl.ds(HALF + member, CX - 2 * PAD, stride=MEM), :
                ]
                out[member, field, :PAD, lanes] = outer[
                    field, part, pl.ds(member, PAD, stride=MEM), :
                ]
                out[member, field, CX - PAD :, lanes] = outer[
                    field, part, pl.ds(HALF + member, PAD, stride=MEM), :
                ]


def spread_out(where, inner, outer):
    return call(spread_out_body, (shaped(MEM, 3, CX, CY),), (where, inner, outer))[0]


def products_body(where, states, own, send, seen_at, wanted_at):
    group = where[0]
    lane = lax.broadcasted_iota(jnp.int32, (1, LANE), 1)

    def unfolded(at):
        value = states[at]
        return jnp.concatenate([value, pltpu.roll(value, LANE // 2, 1)], axis=0)

    left, right = [], []
    for block in range(SUB * 2):
        noisy = [jnp.zeros((MEM, LANE), F32)] * GRP
        other = jnp.zeros((MEM // 2, LANE), F32)
        for source in range(GRP):
            at = 3 * (source * (SUB * 2) + block)
            held, here = unfolded(at + 1), lane // OBS == source
            for part in range(GRP):
                turned = pltpu.roll(held, (source - part) * OBS % LANE, 1)
                noisy[part] = jnp.where(here, turned, noisy[part])
            other = jnp.where(here, pltpu.roll(states[at + 2], source * OBS, 1), other)
        seen = [unfolded(3 * (source * (SUB * 2) + block)) for source in range(GRP)]
        for source in range(GRP):
            wanted_at[block, source] = noisy[source] - seen[source]
            seen_at[block, source] = seen[source]
        seen = [seen_at[block, down_from(group, s)] for s in range(GRP)]
        wanted = [wanted_at[block, up_from(group, s)] for s in range(GRP)]
        seen, wanted = jnp.concatenate(seen, axis=0), jnp.concatenate(wanted, axis=0)
        anomaly = seen - jnp.mean(seen, axis=0, keepdims=True)
        scaled = anomaly / jnp.where(lane < GRP * OBS, other[3:4, :], 1.0)
        left.append(jnp.concatenate([scaled * other[r : r + 1, :] for r in range(3)], axis=0))
        right.append(jnp.concatenate([anomaly, wanted], axis=0))
    products = lax.dot_general(
        jnp.concatenate(left, axis=1),
        jnp.concatenate(right, axis=1),
        (((1,), (1,)), ((), ())),
        precision=HIGHEST,
        preferred_element_type=F32,
    )
    own[...] = products[E : 2 * E, :]
    send[...] = jnp.where(where[1] == 0, products[2 * E :, :], products[:E, :])


def region_products(where, states):
    return call(
        products_body,
        (shaped(E, 2 * E),) * 2,
        (where, states),
        [pltpu.VMEM((SUB * 2, GRP, MEM, LANE), F32)] * 2,
    )


def solve_body(where, own, low, high, out):
    total = own[...] + low[...] + high[...]
    row = lax.broadcasted_iota(jnp.int32, (E, 2 * E), 0)
    lane = lax.broadcasted_iota(jnp.int32, (E, 2 * E), 1)
    system = total + jnp.where(row == lane, E - 1.0, 0.0)
    for k in range(E):
        pivot = system[k : k + 1, :] / system[k : k + 1, k : k + 1]
        system = jnp.where(row == k, pivot, system - system[:, k : k + 1] * pivot)
    out[...] = system[:, E:]


def solve(where, own, low, high):
    return call(solve_body, (shaped(E, E),), (where, own, low, high))[0]


def increments_body(where, weights, *refs):
    blocks, outs = refs[:GRP], refs[GRP:]
    turned = weights[...].T
    coarse = turned.astype(BF16)
    fine = (turned - coarse.astype(F32)).astype(BF16)
    left = jnp.concatenate([coarse, coarse, fine], axis=1)
    for low in range(0, 3 * MIDDLE, HALF):
        pieces = []
        for row in range(PAD):
            at = slice(low + row * MEM, low + (row + 1) * MEM)
            pieces.append(jnp.concatenate([block[at, :] for block in blocks], axis=0))
        state = jnp.concatenate(pieces, axis=1)
        state = state - jnp.mean(state, axis=0, keepdims=True)
        high = state.astype(BF16)
        low_part = (state - high.astype(F32)).astype(BF16)
        right = jnp.concatenate([high, low_part, high], axis=0)
        result = jnp.dot(left, right, preferred_element_type=F32)
        for row in range(PAD):
            for other in range(GRP):
                outs[other][low + row * MEM : low + (row + 1) * MEM, :] = result[
                    other * MEM : (other + 1) * MEM, row * LANE : (row + 1) * LANE
                ]


def increments(where, weights, blocks):
    return call(increments_body, (shaped(3 * MIDDLE, LANE),) * GRP, (where, weights, *blocks))


def exchange(blocks):
    moved = {
        s: lax.ppermute(blocks[s], "grp", [(i, (i + s) % GRP) for i in range(GRP)]) for s in range(1, GRP)
    }
    return [blocks[0]] + [moved[s] for s in range(1, GRP)]


def on_device(
    trial, seabed, observed, variances, perturbations, stencil_cells, stencil_weights, region_mask
):
    group, region = lax.axis_index("grp"), lax.axis_index("reg")
    sub, core = lax.axis_index("sub"), lax.axis_index("cores")
    tile = region * SUB + sub
    where = jnp.stack(
        [group, core, (tile > 0).astype(jnp.int32), (tile < REG * SUB - 1).astype(jnp.int32)]
    ).astype(jnp.int32)
    forward = [(i, i + 1) for i in range(REG * SUB - 1)]
    backward = [(i + 1, i) for i in range(REG * SUB - 1)]

    down, up, beside = pack(where, trial, seabed)
    above = lax.ppermute(down, TILE, forward)
    below = lax.ppermute(up, TILE, backward)
    beside = lax.ppermute(beside, "cores", [(0, 1), (1, 0)])

    count = GRP * OBS
    anchor = stencil_cells[:, 0].astype(F32)
    pair = jnp.stack([anchor, anchor + 1.0])
    uses = stencil_weights.T
    stencil = jnp.stack([pair, uses[:2], uses[2:]])
    slot = (jnp.arange(GRP) == group).astype(F32)
    stencil = (stencil[:, :, None, :] * slot[None, None, :, None]).reshape(3, 2 * count)
    stencil = jnp.pad(stencil, ((0, MEM - 3), (0, 0)))
    noisy = observed[:, None] + jnp.sqrt(variances)[:, None] * perturbations
    noisy = noisy.T.reshape(GRP, 2, MEM // 2, OBS).transpose(2, 1, 0, 3).reshape(MEM // 2, LANE)
    three = lax.dynamic_slice_in_dim(
        jnp.pad(region_mask.astype(F32), ((0, 0), (1, 1))), region, 3, axis=1
    )
    three = jnp.concatenate([three.T, variances[None]], axis=0)
    known = jnp.stack([noisy, jnp.pad(three, ((0, 0), (0, LANE - OBS)))])

    stencil, beside = lax.optimization_barrier((stencil, beside))
    stencils = exchange([stencil] * GRP)
    *middle, inner = inner_forecast(where, trial, seabed, beside)
    above, below, _ = lax.optimization_barrier((above, below, stencils[1:]))

    def outer_rows(above, below, inner, known, stencils):
        edge = jnp.where(core == 0, PARTS - 1, 0)
        ends = [lax.dynamic_index_in_dim(s, edge, 0, keepdims=False) for s in (above, below)]
        corner = lax.ppermute(jnp.stack(ends), "cores", [(0, 1), (1, 0)])
        *outer, state, rest = outer_forecast(
            where, inner, (above, below, corner), known, stencils
        )
        return outer, rest, lax.all_to_all(state, SIDE, 0, 0, tiled=True)

    def nothing(*args):
        block = jnp.zeros((3 * MIDDLE, LANE), F32)
        rest = jnp.zeros((3, PARTS, 2 * HALF, LANE), F32)
        return [block] * GRP, rest, jnp.zeros((3 * GRP * SUB * 2, MEM // 2, LANE), F32)

    middle, *_ = lax.optimization_barrier((middle, stencils[1:]))
    middle = exchange(middle)
    outer, rest, states = lax.cond(
        group < GRP, outer_rows, nothing, above, below, inner, known, stencils
    )
    pairs = [
        (r * SUB + q, (r + 1) * SUB + (q ^ 2)) for r in range(REG - 1) for q in range(SUB)
    ]
    pairs = [(2 * a, 2 * b) for a, b in pairs] + [(2 * b + 1, 2 * a + 1) for a, b in pairs]

    def chain(states):
        own, send = region_products(where, states)
        came = lax.ppermute(send, ("reg", "sub", "cores"), pairs)
        swapped = lax.ppermute(came, "cores", [(0, 1), (1, 0)])
        return solve(where, own, came, swapped)

    states, outer, _ = lax.optimization_barrier((states, outer, middle[1:]))
    outer = exchange(outer)
    propagated_trials = spread_out(where, inner, rest)
    weights = lax.cond(group < GRP, chain, lambda states: jnp.zeros((E, E), F32), states)
    analysis_updates = unpack(
        where,
        exchange(increments(where, weights, middle)),
        exchange(increments(where, weights, outer)),
    )
    return (propagated_trials, analysis_updates)


def solution(mesh):
    fine = Mesh(
        mesh.devices.reshape(GRP, REG, SUB, 2), ("grp", "reg", "sub", "cores")
    )
    every = ("grp", "reg", "sub", "cores")
    state = P("grp", None, TILE, "cores")
    in_specs = (
        state,
        P(TILE, "cores"),
        P(every),
        P(every),
        P(every, None),
        P(every, None),
        P(every, None),
        P(every, None),
    )
    return jax.shard_map(
        on_device, mesh=fine, in_specs=in_specs, out_specs=(state, state), check_vma=False
    )
```

```python
import functools

import jax
import jax.numpy as jnp
from jax import lax
from jax.experimental import pallas as pl
from jax.experimental.pallas import tpu as pltpu
from jax.sharding import Mesh, PartitionSpec as P

STEPS = 3
REG = 8
GRP = 4
SUB = 4
MEM = 8
E = 32
CX = 32
CY = 512
LANE = 128
PARTS = CY // LANE
WIDE = CY + LANE
PAD = 8
OBS = 16
HALF = PAD * MEM
MIDDLE = CX * MEM - 2 * HALF
DU, DV, DL = 4, 5, 5
STRIP = DU + DV + DL + 1
FRICTION = 0.02
HIGHEST = lax.Precision.HIGHEST
F32 = jnp.float32
BF16 = jnp.bfloat16
SIDE = ("grp", "sub", "cores")
TILE = ("reg", "sub")


VMEM = pl.BlockSpec(memory_space=pltpu.VMEM)
SMEM = pl.BlockSpec(memory_space=pltpu.SMEM)
ANY = pl.BlockSpec(memory_space=pl.ANY)


def call(body, outs, args, scratch=(), mib=16, flops=0, moved=0):
    return pl.pallas_call(
        body,
        out_shape=list(outs),
        in_specs=[SMEM] + [VMEM] * (len(args) - 1),
        out_specs=[VMEM] * len(outs),
        scratch_shapes=list(scratch),
        compiler_params=pltpu.CompilerParams(vmem_limit_bytes=mib * 1024 * 1024),
        cost_estimate=pl.CostEstimate(flops=flops, bytes_accessed=moved, transcendentals=0),
    )(*args)


def shaped(*shape, dtype=F32):
    return jax.ShapeDtypeStruct(shape, dtype)


def up_from(group, steps):
    return (group + steps) % GRP


def down_from(group, steps):
    return (group + GRP - steps) % GRP


def aligned(value, unit):
    return pl.multiple_of(value * unit, unit)


def pack_body(where, trial, seabed, down, up, beside, last, first, bed, strips, edges, sems):
    edge = pl.ds(pl.multiple_of(jnp.where(where[1] == 0, CY - LANE, 0), LANE), LANE)
    moves = [
        (trial.at[:, :, CX - PAD :, :], last),
        (seabed, bed),
        (trial.at[:, :, :PAD, :], first),
        (trial.at[:, :, :, edge], edges.at[:MEM]),
        (strips.at[0], down),
        (strips.at[1], up),
        (edges, beside),
    ]
    copies = [pltpu.make_async_copy(*move, sems.at[i]) for i, move in enumerate(moves)]
    for copy in copies[:4]:
        copy.start()
    for side, (rows, end) in enumerate(((last, True), (first, False))):
        if end:
            copies[0].wait()
            copies[1].wait()
        else:
            copies[2].wait()
        base, sign = (CX - PAD, 0.5) if end else (0, -0.5)

        def take(first, count):
            return slice(PAD - first - count, PAD - first) if end else slice(first, first + count)

        for part in range(PARTS):
            lanes = slice(part * LANE, (part + 1) * LANE)
            deep = bed[base : base + PAD, lanes]
            for member in range(MEM):
                level, east, north = (rows[member, f, :, lanes] for f in range(3))

                def put(slot, count, value):
                    to = pl.ds(slot * MEM + member, count, stride=MEM)
                    strips[side, part, to, :] = value

                flux, plus = north * deep, sign * (east * deep)
                near, far = take(3, 2), take(4, 2)
                put(0, DU, east[take(0, DU), :])
                put(DU + end, DV - 1, north[take(0, DV - 1), :])
                put(DU + (0 if end else DV - 1), 1, flux[take(DV - 1, 1), :])
                put(DU + DV + 2 * end, DL - 2, level[take(0, DL - 2), :])
                put(DU + DV + (0 if end else DL - 2), 2, level[near, :] + plus[far, :])
            to = (STRIP - 1) * MEM
            strips[side, part, to : to + MEM, :] = jnp.zeros((MEM, LANE), F32)
            strips[side, part, to : to + DU, :] = deep[take(0, DU), :]
        copies[4 + side].start()
    for same in range(3):
        edges[MEM, same] = bed[:, edge]
    copies[3].wait()
    for copy in copies[6:]:
        copy.start()
    for copy in copies[4:]:
        copy.wait()


def pack(where, trial, seabed):
    strip = shaped(PARTS, STRIP * MEM, LANE)
    rows = pltpu.VMEM((MEM, 3, PAD, CY), F32)
    return pl.pallas_call(
        pack_body,
        out_shape=[strip, strip, shaped(MEM + 1, 3, CX, LANE)],
        in_specs=[SMEM, ANY, ANY],
        out_specs=[ANY] * 3,
        scratch_shapes=[
            rows,
            rows,
            pltpu.VMEM((CX, CY), F32),
            pltpu.VMEM((2,) + strip.shape, F32),
            pltpu.VMEM((MEM + 1, 3, CX, LANE), F32),
            pltpu.SemaphoreType.DMA((7,)),
        ],
        compiler_params=pltpu.CompilerParams(vmem_limit_bytes=60 * 1024 * 1024),
    )(where, trial, seabed)


def row_at(row):
    return pl.ds(aligned(row, MEM), MEM)


def get(ref, row):
    at = row_at(row)
    return jnp.concatenate([ref[part, at, :] for part in range(PARTS + 1)], axis=1)


def put(ref, row, value):
    at = row_at(row)
    for part in range(PARTS + 1):
        ref[part, at, :] = value[:, part * LANE : (part + 1) * LANE]


def across(value):
    return pltpu.roll(value, WIDE - 1, 1) - pltpu.roll(value, 1, 1)


def move_level(fields, row, inside):
    level, east, north, depth = fields
    along = get(depth, row + 1) * get(east, row + 1) - get(depth, row - 1) * get(east, row - 1)
    spread = 0.5 * along + 0.5 * across(get(depth, row) * get(north, row))
    put(level, row, (get(level, row) - spread) * inside)


def move_flow(fields, row):
    level, east, north, _ = fields
    slope = get(level, row + 1) - get(level, row - 1)
    put(east, row, (1.0 - FRICTION) * get(east, row) - 0.5 * slope)
    slope = across(get(level, row))
    put(north, row, (1.0 - FRICTION) * get(north, row) - 0.5 * slope)


def kept_half(core):
    lane = lax.broadcasted_iota(jnp.int32, (1, LANE), 1)
    return jnp.where((lane < LANE // 2) == (core == 0), 1.0, 0.0).astype(F32)


def inside_of(core):
    lane = lax.broadcasted_iota(jnp.int32, (1, WIDE), 1)
    inside = (lane < CY) | ((lane < CY + LANE // 2) == (core == 0))
    return jnp.where(inside, 1.0, 0.0).astype(F32)


def inner_body(where, trial, seabed, beside, *outs):
    blocks, fields = outs[:GRP], [outs[GRP].at[f] for f in range(4)]
    keep, inside = kept_half(where[1]), inside_of(where[1])
    for field in range(3):
        for member in range(MEM):
            at = pl.ds(member, CX, stride=MEM)
            for part in range(PARTS):
                fields[field][part, at, :] = trial[
                    member, field, :, part * LANE : (part + 1) * LANE
                ]
            fields[field][PARTS, at, :] = beside[member, field] * keep
    depth = fields[3]
    for row in range(CX):
        at = slice(row * MEM, (row + 1) * MEM)
        for part in range(PARTS):
            depth[part, at, :] = jnp.broadcast_to(
                seabed[row : row + 1, part * LANE : (part + 1) * LANE], (MEM, LANE)
            )
        depth[PARTS, at, :] = jnp.broadcast_to(
            beside[MEM, 0, row : row + 1, :] * keep, (MEM, LANE)
        )

    def level_row(row, carry):
        move_level(fields, row, inside)
        return carry

    def flow_row(row, carry):
        move_flow(fields, row)
        return carry

    for step in range(STEPS):
        lax.fori_loop(2 * step + 1, CX - 2 * step - 1, level_row, 0, unroll=2)
        lax.fori_loop(2 * step + 2, CX - 2 * step - 2, flow_row, 0, unroll=2)
    for other in range(GRP):
        for field in range(3):
            blocks[other][field * MIDDLE : (field + 1) * MIDDLE, :] = fields[field][
                up_from(where[0], other), HALF : CX * MEM - HALF, :
            ]


def inner_forecast(where, trial, seabed, beside):
    fields = shaped(4, PARTS + 1, CX * MEM, LANE)
    block = shaped(3 * MIDDLE, LANE)
    return call(
        inner_body,
        (block,) * GRP + (fields,),
        (where, trial, seabed, beside),
        flops=10_000_000,
        moved=32_000_000,
    )


def sense(levels, stencils):
    anchor = stencils[0:1, :].astype(jnp.int32)
    lane = lax.broadcasted_iota(jnp.int32, (1, LANE), 1)
    of_group = (lane % (GRP * OBS)) // OBS
    row = anchor // CY + of_group * (CX // GRP)
    pick = lax.broadcasted_iota(jnp.int32, (CY, LANE), 0) == anchor % CY
    pick = jnp.where(pick, 1.0, 0.0).astype(BF16)
    first = levels.astype(BF16)
    left = levels - first.astype(F32)
    second = left.astype(BF16)
    third = (left - second.astype(F32)).astype(BF16)
    dot = functools.partial(jnp.dot, preferred_element_type=F32)
    picked = dot(first, pick) + dot(second, pick) + dot(third, pick)
    total = jnp.zeros((MEM, LANE), F32)
    for at in range(CX):
        here = jnp.where(row == at, stencils[1:2, :], 0.0)
        here += jnp.where(row + 1 == at, stencils[2:3, :], 0.0)
        total += picked[at * MEM : (at + 1) * MEM, :] * here
    return total + pltpu.roll(total, LANE // 2, 1)


def outer_body(where, inner, above, below, corner, known, *rest):
    stencils, rest = rest[:GRP], rest[GRP:]
    blocks, state, whole, scratch = rest[:GRP], rest[GRP], rest[GRP + 1], rest[GRP + 2 :]
    group, core = where[0], where[1]
    keep, inside = kept_half(core), inside_of(core)
    given = [inner.at[f] for f in range(4)]
    half = HALF
    top, bottom = scratch[:4], scratch[4:]
    for field in range(4):
        for part in range(PARTS + 1):
            top[field][part, half:, :] = given[field][part, :half, :]
            bottom[field][part, :half, :] = given[field][part, CX * MEM - half :, :]
    for strip, side, fields in ((above, 0, top), (below, 1, bottom)):
        for part in range(PARTS + 1):

            def piece(low, count):
                if part < PARTS:
                    return strip[part, low : low + count, :]
                return corner[side, low : low + count, :] * keep

            at = 0
            for field, count in ((1, DU), (2, DV), (0, DL)):
                to = half if side else (PAD - count) * MEM
                fields[field][part, to : to + count * MEM, :] = piece(at * MEM, count * MEM)
                at += count
            for row in range(DU):
                to = half + row * MEM if side else (PAD - DU + row) * MEM
                fields[3][part, to : to + MEM, :] = jnp.broadcast_to(
                    piece((STRIP - 1) * MEM + row, 1), (MEM, LANE)
                )
            for beyond in (DU, DU + 1):
                to = half + beyond * MEM if side else half - (beyond + 1) * MEM
                fields[1][part, to : to + MEM, :] = jnp.zeros((MEM, LANE), F32)
                fields[3][part, to : to + MEM, :] = jnp.full((MEM, LANE), 1.0 * (beyond == DU), F32)
    has_above = inside * where[2].astype(F32)
    has_below = inside * where[3].astype(F32)
    for step in range(STEPS):
        shift = 2 * step
        for row in range(-5 + shift, 1 + shift):
            move_level(top, PAD + row, has_above if row < 0 else inside)
            move_level(bottom, PAD - 1 - row, has_below if row < 0 else inside)
        for row in range(-4 + shift, 2 + shift):
            move_flow(top, PAD + row)
            move_flow(bottom, PAD - 1 - row)

    levels = jnp.concatenate(
        [
            jnp.concatenate(
                [
                    top[0][part, half:, :],
                    given[0][part, half : CX * MEM - half, :],
                    bottom[0][part, :half, :],
                ],
                axis=0,
            )
            for part in range(PARTS)
        ],
        axis=1,
    )
    total = sense(levels, sum(s[...] for s in stencils))
    lane = lax.broadcasted_iota(jnp.int32, (1, LANE), 1)
    total = jnp.where(lane < GRP * OBS, total[: MEM // 2, :], total[MEM // 2 :, :])
    for to in range(GRP * SUB * 2):
        state[3 * to] = total
        state[3 * to + 1] = known[0]
        state[3 * to + 2] = known[1]

    for field in range(3):
        for part in range(PARTS):
            whole[field, part, :half, :] = top[field][part, half:, :]
            whole[field, part, half:, :] = bottom[field][part, :half, :]
        for other in range(GRP):
            blocks[other][field * MIDDLE : (field + 1) * MIDDLE, :] = whole[
                field, up_from(group, other)
            ]


def outer_forecast(where, inner, strips, known, stencils):
    block = shaped(3 * MIDDLE, LANE)
    return call(
        outer_body,
        (block,) * GRP
        + (shaped(3 * GRP * SUB * 2, MEM // 2, LANE), shaped(3, PARTS, 2 * HALF, LANE)),
        (where, inner, *strips, known, *stencils),
        [pltpu.VMEM((PARTS + 1, 2 * PAD * MEM, LANE), F32)] * 8,
    )


def unpack_middle_body(where, *refs):
    blocks, out = refs[:GRP], refs[GRP]
    for other, block in enumerate(blocks):
        at = pl.ds(aligned(down_from(where[0], other), LANE), LANE)
        for field in range(3):
            for member in range(MEM):
                out[member, field, PAD : CX - PAD, at] = block[
                    pl.ds(field * MIDDLE + member, CX - 2 * PAD, stride=MEM), :
                ]


def unpack_outer_body(some, where, *refs):
    blocks, (_, out, held, sems) = refs[: len(some)], refs[len(some) :]
    copies = []
    for at, (other, block) in enumerate(zip(some, blocks)):
        lanes = pl.ds(aligned(down_from(where[0], other), LANE), LANE)
        for side, rows in enumerate((pl.ds(0, PAD), pl.ds(CX - PAD, PAD))):
            for field in range(3):
                for member in range(MEM):
                    low = field * MIDDLE + side * HALF + member
                    held[at, side, member, field] = block[pl.ds(low, PAD, stride=MEM), :]
            copies.append(
                pltpu.make_async_copy(
                    held.at[at, side], out.at[:, :, rows, lanes], sems.at[2 * at + side]
                )
            )
            copies[-1].start()
    for copy in copies:
        copy.wait()


def unpack_outer(where, some, blocks, given):
    return pl.pallas_call(
        functools.partial(unpack_outer_body, some),
        out_shape=shaped(MEM, 3, CX, CY),
        in_specs=[SMEM] + [VMEM] * len(some) + [ANY],
        out_specs=ANY,
        scratch_shapes=[
            pltpu.VMEM((len(some), 2, MEM, 3, PAD, LANE), F32),
            pltpu.SemaphoreType.DMA((2 * len(some),)),
        ],
        input_output_aliases={1 + len(some): 0},
        compiler_params=pltpu.CompilerParams(vmem_limit_bytes=16 * 1024 * 1024),
    )(where, *[blocks[s] for s in some], given)


def unpack(where, middle, outer):
    out = shaped(MEM, 3, CX, CY)
    early = call(unpack_middle_body, (out,), (where, *middle), flops=10_000_000, moved=32_000_000)
    early = unpack_outer(where, (0, 1), outer, early[0])
    return unpack_outer(where, (2, 3), outer, early)


def spread_out_body(where, inner, outer, out):
    for part in range(PARTS):
        lanes = slice(part * LANE, (part + 1) * LANE)
        for field in range(3):
            for member in range(MEM):
                out[member, field, PAD : CX - PAD, lanes] = inner[
                    field, part, pl.ds(HALF + member, CX - 2 * PAD, stride=MEM), :
                ]
                out[member, field, :PAD, lanes] = outer[
                    field, part, pl.ds(member, PAD, stride=MEM), :
                ]
                out[member, field, CX - PAD :, lanes] = outer[
                    field, part, pl.ds(HALF + member, PAD, stride=MEM), :
                ]


def spread_out(where, inner, outer):
    return call(spread_out_body, (shaped(MEM, 3, CX, CY),), (where, inner, outer))[0]


def products_body(where, states, own, send, seen_at, wanted_at):
    group = where[0]
    lane = lax.broadcasted_iota(jnp.int32, (1, LANE), 1)

    def unfolded(at):
        value = states[at]
        return jnp.concatenate([value, pltpu.roll(value, LANE // 2, 1)], axis=0)

    left, right = [], []
    for block in range(SUB * 2):
        noisy = [jnp.zeros((MEM, LANE), F32)] * GRP
        other = jnp.zeros((MEM // 2, LANE), F32)
        for source in range(GRP):
            at = 3 * (source * (SUB * 2) + block)
            held, here = unfolded(at + 1), lane // OBS == source
            for part in range(GRP):
                turned = pltpu.roll(held, (source - part) * OBS % LANE, 1)
                noisy[part] = jnp.where(here, turned, noisy[part])
            other = jnp.where(here, pltpu.roll(states[at + 2], source * OBS, 1), other)
        seen = [unfolded(3 * (source * (SUB * 2) + block)) for source in range(GRP)]
        for source in range(GRP):
            wanted_at[block, source] = noisy[source] - seen[source]
            seen_at[block, source] = seen[source]
        seen = [seen_at[block, down_from(group, s)] for s in range(GRP)]
        wanted = [wanted_at[block, up_from(group, s)] for s in range(GRP)]
        seen, wanted = jnp.concatenate(seen, axis=0), jnp.concatenate(wanted, axis=0)
        anomaly = seen - jnp.mean(seen, axis=0, keepdims=True)
        scaled = anomaly / jnp.where(lane < GRP * OBS, other[3:4, :], 1.0)
        left.append(jnp.concatenate([scaled * other[r : r + 1, :] for r in range(3)], axis=0))
        right.append(jnp.concatenate([anomaly, wanted], axis=0))
    products = lax.dot_general(
        jnp.concatenate(left, axis=1),
        jnp.concatenate(right, axis=1),
        (((1,), (1,)), ((), ())),
        precision=HIGHEST,
        preferred_element_type=F32,
    )
    own[...] = products[E : 2 * E, :]
    send[...] = jnp.where(where[1] == 0, products[2 * E :, :], products[:E, :])


def region_products(where, states):
    return call(
        products_body,
        (shaped(E, 2 * E),) * 2,
        (where, states),
        [pltpu.VMEM((SUB * 2, GRP, MEM, LANE), F32)] * 2,
    )


def solve_body(where, own, low, high, out):
    total = own[...] + low[...] + high[...]
    row = lax.broadcasted_iota(jnp.int32, (E, 2 * E), 0)
    lane = lax.broadcasted_iota(jnp.int32, (E, 2 * E), 1)
    system = total + jnp.where(row == lane, E - 1.0, 0.0)
    for k in range(E):
        pivot = system[k : k + 1, :] / system[k : k + 1, k : k + 1]
        system = jnp.where(row == k, pivot, system - system[:, k : k + 1] * pivot)
    out[...] = system[:, E:]


def solve(where, own, low, high):
    return call(solve_body, (shaped(E, E),), (where, own, low, high))[0]


def increments_body(where, weights, *refs):
    blocks, outs = refs[:GRP], refs[GRP:]
    turned = weights[...].T
    coarse = turned.astype(BF16)
    fine = (turned - coarse.astype(F32)).astype(BF16)
    left = jnp.concatenate([coarse, coarse, fine], axis=1)
    for low in range(0, 3 * MIDDLE, HALF):
        pieces = []
        for row in range(PAD):
            at = slice(low + row * MEM, low + (row + 1) * MEM)
            pieces.append(jnp.concatenate([block[at, :] for block in blocks], axis=0))
        state = jnp.concatenate(pieces, axis=1)
        state = state - jnp.mean(state, axis=0, keepdims=True)
        high = state.astype(BF16)
        low_part = (state - high.astype(F32)).astype(BF16)
        right = jnp.concatenate([high, low_part, high], axis=0)
        result = jnp.dot(left, right, preferred_element_type=F32)
        for row in range(PAD):
            for other in range(GRP):
                outs[other][low + row * MEM : low + (row + 1) * MEM, :] = result[
                    other * MEM : (other + 1) * MEM, row * LANE : (row + 1) * LANE
                ]


def increments(where, weights, blocks):
    return call(increments_body, (shaped(3 * MIDDLE, LANE),) * GRP, (where, weights, *blocks))


def exchange(blocks):
    moved = {
        s: lax.ppermute(blocks[s], "grp", [(i, (i + s) % GRP) for i in range(GRP)]) for s in range(1, GRP)
    }
    return [blocks[0]] + [moved[s] for s in range(1, GRP)]


def on_device(
    trial, seabed, observed, variances, perturbations, stencil_cells, stencil_weights, region_mask
):
    group, region = lax.axis_index("grp"), lax.axis_index("reg")
    sub, core = lax.axis_index("sub"), lax.axis_index("cores")
    tile = region * SUB + sub
    where = jnp.stack(
        [group, core, (tile > 0).astype(jnp.int32), (tile < REG * SUB - 1).astype(jnp.int32)]
    ).astype(jnp.int32)
    forward = [(i, i + 1) for i in range(REG * SUB - 1)]
    backward = [(i + 1, i) for i in range(REG * SUB - 1)]

    down, up, beside = pack(where, trial, seabed)
    above = lax.ppermute(down, TILE, forward)
    below = lax.ppermute(up, TILE, backward)
    beside = lax.ppermute(beside, "cores", [(0, 1), (1, 0)])

    count = GRP * OBS
    anchor = stencil_cells[:, 0].astype(F32)
    pair = jnp.stack([anchor, anchor + 1.0])
    uses = stencil_weights.T
    stencil = jnp.stack([pair, uses[:2], uses[2:]])
    slot = (jnp.arange(GRP) == group).astype(F32)
    stencil = (stencil[:, :, None, :] * slot[None, None, :, None]).reshape(3, 2 * count)
    stencil = jnp.pad(stencil, ((0, MEM - 3), (0, 0)))
    noisy = observed[:, None] + jnp.sqrt(variances)[:, None] * perturbations
    noisy = noisy.T.reshape(GRP, 2, MEM // 2, OBS).transpose(2, 1, 0, 3).reshape(MEM // 2, LANE)
    three = lax.dynamic_slice_in_dim(
        jnp.pad(region_mask.astype(F32), ((0, 0), (1, 1))), region, 3, axis=1
    )
    three = jnp.concatenate([three.T, variances[None]], axis=0)
    known = jnp.stack([noisy, jnp.pad(three, ((0, 0), (0, LANE - OBS)))])

    stencil, beside = lax.optimization_barrier((stencil, beside))
    stencils = exchange([stencil] * GRP)
    *middle, inner = inner_forecast(where, trial, seabed, beside)
    above, below, _ = lax.optimization_barrier((above, below, stencils[1:]))

    def outer_rows(above, below, inner, known, stencils):
        edge = jnp.where(core == 0, PARTS - 1, 0)
        ends = [lax.dynamic_index_in_dim(s, edge, 0, keepdims=False) for s in (above, below)]
        corner = lax.ppermute(jnp.stack(ends), "cores", [(0, 1), (1, 0)])
        *outer, state, rest = outer_forecast(
            where, inner, (above, below, corner), known, stencils
        )
        return outer, rest, lax.all_to_all(state, SIDE, 0, 0, tiled=True)

    def nothing(*args):
        block = jnp.zeros((3 * MIDDLE, LANE), F32)
        rest = jnp.zeros((3, PARTS, 2 * HALF, LANE), F32)
        return [block] * GRP, rest, jnp.zeros((3 * GRP * SUB * 2, MEM // 2, LANE), F32)

    middle, *_ = lax.optimization_barrier((middle, stencils[1:]))
    middle = exchange(middle)
    outer, rest, states = lax.cond(
        group < GRP, outer_rows, nothing, above, below, inner, known, stencils
    )
    pairs = [
        (r * SUB + q, (r + 1) * SUB + (q ^ 2)) for r in range(REG - 1) for q in range(SUB)
    ]
    pairs = [(2 * a, 2 * b) for a, b in pairs] + [(2 * b + 1, 2 * a + 1) for a, b in pairs]

    def chain(states):
        own, send = region_products(where, states)
        came = lax.ppermute(send, ("reg", "sub", "cores"), pairs)
        swapped = lax.ppermute(came, "cores", [(0, 1), (1, 0)])
        return solve(where, own, came, swapped)

    states, outer, _ = lax.optimization_barrier((states, outer, middle[1:]))
    outer = exchange(outer)
    propagated_trials = spread_out(where, inner, rest)
    weights = lax.cond(group < GRP, chain, lambda states: jnp.zeros((E, E), F32), states)
    analysis_updates = unpack(
        where,
        exchange(increments(where, weights, middle)),
        exchange(increments(where, weights, outer)),
    )
    return (propagated_trials, analysis_updates)


def solution(mesh):
    fine = Mesh(
        mesh.devices.reshape(GRP, REG, SUB, 2), ("grp", "reg", "sub", "cores")
    )
    every = ("grp", "reg", "sub", "cores")
    state = P("grp", None, TILE, "cores")
    in_specs = (
        state,
        P(TILE, "cores"),
        P(every),
        P(every),
        P(every, None),
        P(every, None),
        P(every, None),
        P(every, None),
    )
    return jax.shard_map(
        on_device, mesh=fine, in_specs=in_specs, out_specs=(state, state), check_vma=False
    )
```

```python
import functools

import jax
import jax.numpy as jnp
from jax import lax
from jax.experimental import pallas as pl
from jax.experimental.pallas import tpu as pltpu
from jax.sharding import Mesh, PartitionSpec as P

STEPS = 3
REG = 8
GRP = 4
SUB = 4
MEM = 8
E = 32
CX = 32
CY = 512
LANE = 128
PARTS = CY // LANE
WIDE = CY + LANE
PAD = 8
OBS = 16
HALF = PAD * MEM
MIDDLE = CX * MEM - 2 * HALF
DU, DV, DL = 4, 5, 5
STRIP = DU + DV + DL + 1
FRICTION = 0.02
HIGHEST = lax.Precision.HIGHEST
F32 = jnp.float32
BF16 = jnp.bfloat16
SIDE = ("grp", "sub", "cores")
TILE = ("reg", "sub")


VMEM = pl.BlockSpec(memory_space=pltpu.VMEM)
SMEM = pl.BlockSpec(memory_space=pltpu.SMEM)
ANY = pl.BlockSpec(memory_space=pl.ANY)


def call(body, outs, args, scratch=(), mib=16, flops=0, moved=0):
    return pl.pallas_call(
        body,
        out_shape=list(outs),
        in_specs=[SMEM] + [VMEM] * (len(args) - 1),
        out_specs=[VMEM] * len(outs),
        scratch_shapes=list(scratch),
        compiler_params=pltpu.CompilerParams(vmem_limit_bytes=mib * 1024 * 1024),
        cost_estimate=pl.CostEstimate(flops=flops, bytes_accessed=moved, transcendentals=0),
    )(*args)


def shaped(*shape, dtype=F32):
    return jax.ShapeDtypeStruct(shape, dtype)


def up_from(group, steps):
    return (group + steps) % GRP


def down_from(group, steps):
    return (group + GRP - steps) % GRP


def aligned(value, unit):
    return pl.multiple_of(value * unit, unit)


def pack_body(where, trial, seabed, down, up, beside, last, first, bed, strips, edges, sems):
    edge = pl.ds(pl.multiple_of(jnp.where(where[1] == 0, CY - LANE, 0), LANE), LANE)
    moves = [
        (trial.at[:, :, CX - PAD :, :], last),
        (seabed, bed),
        (trial.at[:, :, :PAD, :], first),
        (trial.at[:, :, :, edge], edges.at[:MEM]),
        (strips.at[0], down),
        (strips.at[1], up),
        (edges, beside),
    ]
    copies = [pltpu.make_async_copy(*move, sems.at[i]) for i, move in enumerate(moves)]
    for copy in copies[:4]:
        copy.start()
    for side, (rows, end) in enumerate(((last, True), (first, False))):
        if end:
            copies[0].wait()
            copies[1].wait()
        else:
            copies[2].wait()
        base, sign = (CX - PAD, 0.5) if end else (0, -0.5)

        def take(first, count):
            return slice(PAD - first - count, PAD - first) if end else slice(first, first + count)

        for part in range(PARTS):
            lanes = slice(part * LANE, (part + 1) * LANE)
            deep = bed[base : base + PAD, lanes]
            for member in range(MEM):
                level, east, north = (rows[member, f, :, lanes] for f in range(3))

                def put(slot, count, value):
                    to = pl.ds(slot * MEM + member, count, stride=MEM)
                    strips[side, part, to, :] = value

                flux, plus = north * deep, sign * (east * deep)
                near, far = take(3, 2), take(4, 2)
                put(0, DU, east[take(0, DU), :])
                put(DU + end, DV - 1, north[take(0, DV - 1), :])
                put(DU + (0 if end else DV - 1), 1, flux[take(DV - 1, 1), :])
                put(DU + DV + 2 * end, DL - 2, level[take(0, DL - 2), :])
                put(DU + DV + (0 if end else DL - 2), 2, level[near, :] + plus[far, :])
            to = (STRIP - 1) * MEM
            strips[side, part, to : to + MEM, :] = jnp.zeros((MEM, LANE), F32)
            strips[side, part, to : to + DU, :] = deep[take(0, DU), :]
        copies[4 + side].start()
    for same in range(3):
        edges[MEM, same] = bed[:, edge]
    copies[3].wait()
    for copy in copies[6:]:
        copy.start()
    for copy in copies[4:]:
        copy.wait()


def pack(where, trial, seabed):
    strip = shaped(PARTS, STRIP * MEM, LANE)
    rows = pltpu.VMEM((MEM, 3, PAD, CY), F32)
    return pl.pallas_call(
        pack_body,
        out_shape=[strip, strip, shaped(MEM + 1, 3, CX, LANE)],
        in_specs=[SMEM, ANY, ANY],
        out_specs=[ANY] * 3,
        scratch_shapes=[
            rows,
            rows,
            pltpu.VMEM((CX, CY), F32),
            pltpu.VMEM((2,) + strip.shape, F32),
            pltpu.VMEM((MEM + 1, 3, CX, LANE), F32),
            pltpu.SemaphoreType.DMA((7,)),
        ],
        compiler_params=pltpu.CompilerParams(vmem_limit_bytes=60 * 1024 * 1024),
    )(where, trial, seabed)


def row_at(row):
    return pl.ds(aligned(row, MEM), MEM)


def get(ref, row):
    at = row_at(row)
    return jnp.concatenate([ref[part, at, :] for part in range(PARTS + 1)], axis=1)


def put(ref, row, value):
    at = row_at(row)
    for part in range(PARTS + 1):
        ref[part, at, :] = value[:, part * LANE : (part + 1) * LANE]


def across(value):
    return pltpu.roll(value, WIDE - 1, 1) - pltpu.roll(value, 1, 1)


def move_level(fields, row, inside):
    level, east, north, depth = fields
    along = get(depth, row + 1) * get(east, row + 1) - get(depth, row - 1) * get(east, row - 1)
    spread = 0.5 * along + 0.5 * across(get(depth, row) * get(north, row))
    put(level, row, (get(level, row) - spread) * inside)


def move_flow(fields, row):
    level, east, north, _ = fields
    slope = get(level, row + 1) - get(level, row - 1)
    put(east, row, (1.0 - FRICTION) * get(east, row) - 0.5 * slope)
    slope = across(get(level, row))
    put(north, row, (1.0 - FRICTION) * get(north, row) - 0.5 * slope)


def kept_half(core):
    lane = lax.broadcasted_iota(jnp.int32, (1, LANE), 1)
    return jnp.where((lane < LANE // 2) == (core == 0), 1.0, 0.0).astype(F32)


def inside_of(core):
    lane = lax.broadcasted_iota(jnp.int32, (1, WIDE), 1)
    inside = (lane < CY) | ((lane < CY + LANE // 2) == (core == 0))
    return jnp.where(inside, 1.0, 0.0).astype(F32)


def inner_body(where, trial, seabed, beside, *outs):
    blocks, fields = outs[:GRP], [outs[GRP].at[f] for f in range(4)]
    keep, inside = kept_half(where[1]), inside_of(where[1])
    for field in range(3):
        for member in range(MEM):
            at = pl.ds(member, CX, stride=MEM)
            for part in range(PARTS):
                fields[field][part, at, :] = trial[
                    member, field, :, part * LANE : (part + 1) * LANE
                ]
            fields[field][PARTS, at, :] = beside[member, field] * keep
    depth = fields[3]
    for row in range(CX):
        at = slice(row * MEM, (row + 1) * MEM)
        for part in range(PARTS):
            depth[part, at, :] = jnp.broadcast_to(
                seabed[row : row + 1, part * LANE : (part + 1) * LANE], (MEM, LANE)
            )
        depth[PARTS, at, :] = jnp.broadcast_to(
            beside[MEM, 0, row : row + 1, :] * keep, (MEM, LANE)
        )

    def level_row(row, carry):
        move_level(fields, row, inside)
        return carry

    def flow_row(row, carry):
        move_flow(fields, row)
        return carry

    for step in range(STEPS):
        lax.fori_loop(2 * step + 1, CX - 2 * step - 1, level_row, 0, unroll=2)
        lax.fori_loop(2 * step + 2, CX - 2 * step - 2, flow_row, 0, unroll=2)
    for other in range(GRP):
        for field in range(3):
            blocks[other][field * MIDDLE : (field + 1) * MIDDLE, :] = fields[field][
                up_from(where[0], other), HALF : CX * MEM - HALF, :
            ]


def inner_forecast(where, trial, seabed, beside):
    fields = shaped(4, PARTS + 1, CX * MEM, LANE)
    block = shaped(3 * MIDDLE, LANE)
    return call(
        inner_body,
        (block,) * GRP + (fields,),
        (where, trial, seabed, beside),
        flops=10_000_000,
        moved=32_000_000,
    )


def sense(levels, stencils):
    anchor = stencils[0:1, :].astype(jnp.int32)
    lane = lax.broadcasted_iota(jnp.int32, (1, LANE), 1)
    of_group = (lane % (GRP * OBS)) // OBS
    row = anchor // CY + of_group * (CX // GRP)
    pick = lax.broadcasted_iota(jnp.int32, (CY, LANE), 0) == anchor % CY
    pick = jnp.where(pick, 1.0, 0.0).astype(BF16)
    first = levels.astype(BF16)
    left = levels - first.astype(F32)
    second = left.astype(BF16)
    third = (left - second.astype(F32)).astype(BF16)
    parts = jnp.concatenate([first, second, third], axis=1)
    picked = jnp.dot(
        parts, jnp.concatenate([pick] * 3, axis=0), preferred_element_type=F32
    )
    total = jnp.zeros((MEM, LANE), F32)
    for at in range(CX):
        here = jnp.where(row == at, stencils[1:2, :], 0.0)
        here += jnp.where(row + 1 == at, stencils[2:3, :], 0.0)
        total += picked[at * MEM : (at + 1) * MEM, :] * here
    return total + pltpu.roll(total, LANE // 2, 1)


def outer_body(where, inner, above, below, corner, known, *rest):
    stencils, rest = rest[:GRP], rest[GRP:]
    blocks, state, whole, scratch = rest[:GRP], rest[GRP], rest[GRP + 1], rest[GRP + 2 :]
    group, core = where[0], where[1]
    keep, inside = kept_half(core), inside_of(core)
    given = [inner.at[f] for f in range(4)]
    half = HALF
    top, bottom = scratch[:4], scratch[4:]
    for field in range(4):
        for part in range(PARTS + 1):
            top[field][part, half:, :] = given[field][part, :half, :]
            bottom[field][part, :half, :] = given[field][part, CX * MEM - half :, :]
    for strip, side, fields in ((above, 0, top), (below, 1, bottom)):
        for part in range(PARTS + 1):

            def piece(low, count):
                if part < PARTS:
                    return strip[part, low : low + count, :]
                return corner[side, low : low + count, :] * keep

            at = 0
            for field, count in ((1, DU), (2, DV), (0, DL)):
                to = half if side else (PAD - count) * MEM
                fields[field][part, to : to + count * MEM, :] = piece(at * MEM, count * MEM)
                at += count
            for row in range(DU):
                to = half + row * MEM if side else (PAD - DU + row) * MEM
                fields[3][part, to : to + MEM, :] = jnp.broadcast_to(
                    piece((STRIP - 1) * MEM + row, 1), (MEM, LANE)
                )
            for beyond in (DU, DU + 1):
                to = half + beyond * MEM if side else half - (beyond + 1) * MEM
                fields[1][part, to : to + MEM, :] = jnp.zeros((MEM, LANE), F32)
                fields[3][part, to : to + MEM, :] = jnp.full((MEM, LANE), 1.0 * (beyond == DU), F32)
    has_above = inside * where[2].astype(F32)
    has_below = inside * where[3].astype(F32)
    for step in range(STEPS):
        shift = 2 * step
        for row in range(-5 + shift, 1 + shift):
            move_level(top, PAD + row, has_above if row < 0 else inside)
            move_level(bottom, PAD - 1 - row, has_below if row < 0 else inside)
        for row in range(-4 + shift, 2 + shift):
            move_flow(top, PAD + row)
            move_flow(bottom, PAD - 1 - row)

    levels = jnp.concatenate(
        [
            jnp.concatenate(
                [
                    top[0][part, half:, :],
                    given[0][part, half : CX * MEM - half, :],
                    bottom[0][part, :half, :],
                ],
                axis=0,
            )
            for part in range(PARTS)
        ],
        axis=1,
    )
    total = sense(levels, sum(s[...] for s in stencils))
    lane = lax.broadcasted_iota(jnp.int32, (1, LANE), 1)
    total = jnp.where(lane < GRP * OBS, total[: MEM // 2, :], total[MEM // 2 :, :])
    for to in range(GRP * SUB * 2):
        state[3 * to] = total
        state[3 * to + 1] = known[0]
        state[3 * to + 2] = known[1]

    for field in range(3):
        for part in range(PARTS):
            whole[field, part, :half, :] = top[field][part, half:, :]
            whole[field, part, half:, :] = bottom[field][part, :half, :]
        for other in range(GRP):
            blocks[other][field * MIDDLE : (field + 1) * MIDDLE, :] = whole[
                field, up_from(group, other)
            ]


def outer_forecast(where, inner, strips, known, stencils):
    block = shaped(3 * MIDDLE, LANE)
    return call(
        outer_body,
        (block,) * GRP
        + (shaped(3 * GRP * SUB * 2, MEM // 2, LANE), shaped(3, PARTS, 2 * HALF, LANE)),
        (where, inner, *strips, known, *stencils),
        [pltpu.VMEM((PARTS + 1, 2 * PAD * MEM, LANE), F32)] * 8,
    )


def unpack_middle_body(where, *refs):
    blocks, out = refs[:GRP], refs[GRP]
    for other, block in enumerate(blocks):
        at = pl.ds(aligned(down_from(where[0], other), LANE), LANE)
        for field in range(3):
            for member in range(MEM):
                out[member, field, PAD : CX - PAD, at] = block[
                    pl.ds(field * MIDDLE + member, CX - 2 * PAD, stride=MEM), :
                ]


def unpack_outer_body(some, where, *refs):
    blocks, (_, out, held, sems) = refs[: len(some)], refs[len(some) :]
    copies = []
    for at, (other, block) in enumerate(zip(some, blocks)):
        lanes = pl.ds(aligned(down_from(where[0], other), LANE), LANE)
        for side, rows in enumerate((pl.ds(0, PAD), pl.ds(CX - PAD, PAD))):
            for field in range(3):
                for member in range(MEM):
                    low = field * MIDDLE + side * HALF + member
                    held[at, side, member, field] = block[pl.ds(low, PAD, stride=MEM), :]
            copies.append(
                pltpu.make_async_copy(
                    held.at[at, side], out.at[:, :, rows, lanes], sems.at[2 * at + side]
                )
            )
            copies[-1].start()
    for copy in copies:
        copy.wait()


def unpack_outer(where, some, blocks, given):
    return pl.pallas_call(
        functools.partial(unpack_outer_body, some),
        out_shape=shaped(MEM, 3, CX, CY),
        in_specs=[SMEM] + [VMEM] * len(some) + [ANY],
        out_specs=ANY,
        scratch_shapes=[
            pltpu.VMEM((len(some), 2, MEM, 3, PAD, LANE), F32),
            pltpu.SemaphoreType.DMA((2 * len(some),)),
        ],
        input_output_aliases={1 + len(some): 0},
        compiler_params=pltpu.CompilerParams(vmem_limit_bytes=16 * 1024 * 1024),
    )(where, *[blocks[s] for s in some], given)


def unpack(where, middle, outer):
    out = shaped(MEM, 3, CX, CY)
    early = call(unpack_middle_body, (out,), (where, *middle), flops=10_000_000, moved=32_000_000)
    early = unpack_outer(where, (0, 1), outer, early[0])
    return unpack_outer(where, (2, 3), outer, early)


def spread_out_body(where, inner, outer, out):
    for part in range(PARTS):
        lanes = slice(part * LANE, (part + 1) * LANE)
        for field in range(3):
            for member in range(MEM):
                out[member, field, PAD : CX - PAD, lanes] = inner[
                    field, part, pl.ds(HALF + member, CX - 2 * PAD, stride=MEM), :
                ]
                out[member, field, :PAD, lanes] = outer[
                    field, part, pl.ds(member, PAD, stride=MEM), :
                ]
                out[member, field, CX - PAD :, lanes] = outer[
                    field, part, pl.ds(HALF + member, PAD, stride=MEM), :
                ]


def spread_out(where, inner, outer):
    return call(spread_out_body, (shaped(MEM, 3, CX, CY),), (where, inner, outer))[0]


def products_body(where, states, own, send, seen_at, wanted_at):
    group = where[0]
    lane = lax.broadcasted_iota(jnp.int32, (1, LANE), 1)

    def unfolded(at):
        value = states[at]
        return jnp.concatenate([value, pltpu.roll(value, LANE // 2, 1)], axis=0)

    left, right = [], []
    for block in range(SUB * 2):
        noisy = [jnp.zeros((MEM, LANE), F32)] * GRP
        other = jnp.zeros((MEM // 2, LANE), F32)
        for source in range(GRP):
            at = 3 * (source * (SUB * 2) + block)
            held, here = unfolded(at + 1), lane // OBS == source
            for part in range(GRP):
                turned = pltpu.roll(held, (source - part) * OBS % LANE, 1)
                noisy[part] = jnp.where(here, turned, noisy[part])
            other = jnp.where(here, pltpu.roll(states[at + 2], source * OBS, 1), other)
        seen = [unfolded(3 * (source * (SUB * 2) + block)) for source in range(GRP)]
        for source in range(GRP):
            wanted_at[block, source] = noisy[source] - seen[source]
            seen_at[block, source] = seen[source]
        seen = [seen_at[block, down_from(group, s)] for s in range(GRP)]
        wanted = [wanted_at[block, up_from(group, s)] for s in range(GRP)]
        seen, wanted = jnp.concatenate(seen, axis=0), jnp.concatenate(wanted, axis=0)
        anomaly = seen - jnp.mean(seen, axis=0, keepdims=True)
        scaled = anomaly / jnp.where(lane < GRP * OBS, other[3:4, :], 1.0)
        left.append(jnp.concatenate([scaled * other[r : r + 1, :] for r in range(3)], axis=0))
        right.append(jnp.concatenate([anomaly, wanted], axis=0))
    products = lax.dot_general(
        jnp.concatenate(left, axis=1),
        jnp.concatenate(right, axis=1),
        (((1,), (1,)), ((), ())),
        precision=HIGHEST,
        preferred_element_type=F32,
    )
    own[...] = products[E : 2 * E, :]
    send[...] = jnp.where(where[1] == 0, products[2 * E :, :], products[:E, :])


def region_products(where, states):
    return call(
        products_body,
        (shaped(E, 2 * E),) * 2,
        (where, states),
        [pltpu.VMEM((SUB * 2, GRP, MEM, LANE), F32)] * 2,
    )


def solve_body(where, own, low, high, out):
    total = own[...] + low[...] + high[...]
    row = lax.broadcasted_iota(jnp.int32, (E, 2 * E), 0)
    lane = lax.broadcasted_iota(jnp.int32, (E, 2 * E), 1)
    system = total + jnp.where(row == lane, E - 1.0, 0.0)
    for k in range(E):
        pivot = system[k : k + 1, :] / system[k : k + 1, k : k + 1]
        system = jnp.where(row == k, pivot, system - system[:, k : k + 1] * pivot)
    out[...] = system[:, E:]


def solve(where, own, low, high):
    return call(solve_body, (shaped(E, E),), (where, own, low, high))[0]


def increments_body(where, weights, *refs):
    blocks, outs = refs[:GRP], refs[GRP:]
    turned = weights[...].T
    coarse = turned.astype(BF16)
    fine = (turned - coarse.astype(F32)).astype(BF16)
    left = jnp.concatenate([coarse, coarse, fine], axis=1)
    for low in range(0, 3 * MIDDLE, HALF):
        pieces = []
        for row in range(PAD):
            at = slice(low + row * MEM, low + (row + 1) * MEM)
            pieces.append(jnp.concatenate([block[at, :] for block in blocks], axis=0))
        state = jnp.concatenate(pieces, axis=1)
        state = state - jnp.mean(state, axis=0, keepdims=True)
        high = state.astype(BF16)
        low_part = (state - high.astype(F32)).astype(BF16)
        right = jnp.concatenate([high, low_part, high], axis=0)
        result = jnp.dot(left, right, preferred_element_type=F32)
        for row in range(PAD):
            for other in range(GRP):
                outs[other][low + row * MEM : low + (row + 1) * MEM, :] = result[
                    other * MEM : (other + 1) * MEM, row * LANE : (row + 1) * LANE
                ]


def increments(where, weights, blocks):
    return call(increments_body, (shaped(3 * MIDDLE, LANE),) * GRP, (where, weights, *blocks))


def exchange(blocks):
    moved = {
        s: lax.ppermute(blocks[s], "grp", [(i, (i + s) % GRP) for i in range(GRP)]) for s in range(1, GRP)
    }
    return [blocks[0]] + [moved[s] for s in range(1, GRP)]


def on_device(
    trial, seabed, observed, variances, perturbations, stencil_cells, stencil_weights, region_mask
):
    group, region = lax.axis_index("grp"), lax.axis_index("reg")
    sub, core = lax.axis_index("sub"), lax.axis_index("cores")
    tile = region * SUB + sub
    where = jnp.stack(
        [group, core, (tile > 0).astype(jnp.int32), (tile < REG * SUB - 1).astype(jnp.int32)]
    ).astype(jnp.int32)
    forward = [(i, i + 1) for i in range(REG * SUB - 1)]
    backward = [(i + 1, i) for i in range(REG * SUB - 1)]

    down, up, beside = pack(where, trial, seabed)
    above = lax.ppermute(down, TILE, forward)
    below = lax.ppermute(up, TILE, backward)
    beside = lax.ppermute(beside, "cores", [(0, 1), (1, 0)])

    count = GRP * OBS
    anchor = stencil_cells[:, 0].astype(F32)
    pair = jnp.stack([anchor, anchor + 1.0])
    uses = stencil_weights.T
    stencil = jnp.stack([pair, uses[:2], uses[2:]])
    slot = (jnp.arange(GRP) == group).astype(F32)
    stencil = (stencil[:, :, None, :] * slot[None, None, :, None]).reshape(3, 2 * count)
    stencil = jnp.pad(stencil, ((0, MEM - 3), (0, 0)))
    noisy = observed[:, None] + jnp.sqrt(variances)[:, None] * perturbations
    noisy = noisy.T.reshape(GRP, 2, MEM // 2, OBS).transpose(2, 1, 0, 3).reshape(MEM // 2, LANE)
    three = lax.dynamic_slice_in_dim(
        jnp.pad(region_mask.astype(F32), ((0, 0), (1, 1))), region, 3, axis=1
    )
    three = jnp.concatenate([three.T, variances[None]], axis=0)
    known = jnp.stack([noisy, jnp.pad(three, ((0, 0), (0, LANE - OBS)))])

    stencil, beside = lax.optimization_barrier((stencil, beside))
    stencils = exchange([stencil] * GRP)
    *middle, inner = inner_forecast(where, trial, seabed, beside)
    above, below, _ = lax.optimization_barrier((above, below, stencils[1:]))

    def outer_rows(above, below, inner, known, stencils):
        edge = jnp.where(core == 0, PARTS - 1, 0)
        ends = [lax.dynamic_index_in_dim(s, edge, 0, keepdims=False) for s in (above, below)]
        corner = lax.ppermute(jnp.stack(ends), "cores", [(0, 1), (1, 0)])
        *outer, state, rest = outer_forecast(
            where, inner, (above, below, corner), known, stencils
        )
        return outer, rest, lax.all_to_all(state, SIDE, 0, 0, tiled=True)

    def nothing(*args):
        block = jnp.zeros((3 * MIDDLE, LANE), F32)
        rest = jnp.zeros((3, PARTS, 2 * HALF, LANE), F32)
        return [block] * GRP, rest, jnp.zeros((3 * GRP * SUB * 2, MEM // 2, LANE), F32)

    middle, *_ = lax.optimization_barrier((middle, stencils[1:]))
    middle = exchange(middle)
    outer, rest, states = lax.cond(
        group < GRP, outer_rows, nothing, above, below, inner, known, stencils
    )
    pairs = [
        (r * SUB + q, (r + 1) * SUB + (q ^ 2)) for r in range(REG - 1) for q in range(SUB)
    ]
    pairs = [(2 * a, 2 * b) for a, b in pairs] + [(2 * b + 1, 2 * a + 1) for a, b in pairs]

    def chain(states):
        own, send = region_products(where, states)
        came = lax.ppermute(send, ("reg", "sub", "cores"), pairs)
        swapped = lax.ppermute(came, "cores", [(0, 1), (1, 0)])
        return solve(where, own, came, swapped)

    states, outer, _ = lax.optimization_barrier((states, outer, middle[1:]))
    outer = exchange(outer)
    propagated_trials = spread_out(where, inner, rest)
    weights = lax.cond(group < GRP, chain, lambda states: jnp.zeros((E, E), F32), states)
    analysis_updates = unpack(
        where,
        exchange(increments(where, weights, middle)),
        exchange(increments(where, weights, outer)),
    )
    return (propagated_trials, analysis_updates)


def solution(mesh):
    fine = Mesh(
        mesh.devices.reshape(GRP, REG, SUB, 2), ("grp", "reg", "sub", "cores")
    )
    every = ("grp", "reg", "sub", "cores")
    state = P("grp", None, TILE, "cores")
    in_specs = (
        state,
        P(TILE, "cores"),
        P(every),
        P(every),
        P(every, None),
        P(every, None),
        P(every, None),
        P(every, None),
    )
    return jax.shard_map(
        on_device, mesh=fine, in_specs=in_specs, out_specs=(state, state), check_vma=False
    )
```
